256 devices in a mesh: role: 2 (over core), grp: 8 (over z), tp: 16 (over y, x).
Axes of the slice: x: 4, y: 4, z: 8, core: 2. Of those that a mesh axis runs over, the one named last changes fastest.
Arguments:
- queries: bfloat16 [2048, 3072], P(('grp', 'tp')), may hold values from -96 to 96
- cached_keys: bfloat16 [2048, 128, 512], P(('grp', 'tp')), may hold values from -4 to 4
- cached_values: bfloat16 [2048, 128, 512], P(('grp', 'tp')), may hold values from -6 to 6
- lengths: int32 [2048], P(('grp', 'tp')), may hold values from 2 to 128, as said below
- norm_gain: float32 [3072], replicated, may hold values from 0.25 to 1.75
- expert_ids: int32 [2048, 2], P(('grp', 'tp')), may hold values from 0 to 7, all different within a row; in each aligned block of 16 rows (0 to 15, 16 to 31, ...) at most 8 rows name the same one
- gates: float32 [2048, 2], P(('grp', 'tp')), may hold values from 0.1 to 1
- gate_proj: bfloat16 [8, 3072, 8192], P('grp', None, 'tp'), may hold values from -0.109375 to 0.109375
- up_proj: bfloat16 [8, 3072, 8192], P('grp', None, 'tp'), may hold values from -0.109375 to 0.109375
- down_proj: bfloat16 [8, 8192, 3072], P('grp', 'tp'), may hold values from -0.0625 to 0.0625
Outputs:
- mixed: bfloat16 [2048, 3072], P(('grp', 'tp'), 'role')
The draws below stay inside these ranges and needn't reach their ends.
Inputs may be any that keep to these rules, and one draw needn't show every extreme that they name: `expert_ids`: each row names two different experts. Among the 16 rows of one attention device (aligned blocks) no expert is named by more than 8 rows, and some block has an expert named by exactly 8 rows. `lengths`: some request has all 128 positions valid.
All inputs are finite; a program needn't handle non-finite values.
Results may differ from the reference program's by a relative error of at most 0.02.
Values may be sent and summed in bfloat16 or wider, within the bound.
A program may use at most 64 MiB of HBM per device.

```python
import math
import jax
import jax.numpy as jnp
import numpy as np
from jax import lax

HEAD_WIDTH = 128
QUERY_HEADS = 24
KEY_VALUE_HEADS = 4
MODEL_WIDTH = 3072
FF = 8192
DEVICE_REQUESTS = 16
CACHE_SLOTS = 128
EXPERTS = 8
MOST = 8
REQUEST_TOTAL = 2048
N_GRP = 8
N_TP = 16


def key_base(key):
    return jnp.clip(jax.random.normal(key, (REQUEST_TOTAL, CACHE_SLOTS, KEY_VALUE_HEADS * HEAD_WIDTH), jnp.float32), -4.0, 4.0)


def draw_cached_keys(key, part):
    start_offset = key_base(key)
    return start_offset.astype(jnp.bfloat16)


def draw_queries(key, part):
    key = jax.random.fold_in(key, 7)
    values = jax.random.normal(key, (REQUEST_TOTAL, QUERY_HEADS, HEAD_WIDTH), jnp.float32)
    return values.reshape(REQUEST_TOTAL, QUERY_HEADS * HEAD_WIDTH).astype(jnp.bfloat16)


def draw_lengths(key, part):
    key = jax.random.fold_in(key, 5)
    first_key, second_key = jax.random.split(key)
    start_offset = jax.random.randint(first_key, (REQUEST_TOTAL,), 2, CACHE_SLOTS + 1)
    picked = jax.random.randint(second_key, (), 0, REQUEST_TOTAL)
    return jnp.where(jnp.arange(REQUEST_TOTAL) == picked, CACHE_SLOTS, start_offset).astype(jnp.int32)


def block_scale(key, shape, cuts, least, largest):
    gain = 1.0
    for position, parts in cuts:
        steps = jax.random.uniform(jax.random.fold_in(jax.random.fold_in(key, 6), position), (parts,), jnp.float32, least / len(cuts), largest / len(cuts))
        gain = gain * jnp.repeat(jnp.exp(steps), shape[position] // parts).reshape((-1,) + (1,) * (len(shape) - 1 - position))
    return gain


def deal_out(own_key, own, number, rows, count, top, most, lean):
    sequence = jax.random.permutation(own_key, count)
    packed, ordinary = shares(count, rows * top, most, lean, True), shares(count, rows * top, most, lean, False)
    places = jnp.arange(count)

    def named(tallies, rotation):
        used = int((tallies > 0).sum())
        fixed = max(1, used // 4)
        moved = fixed + (places - fixed + rotation * (used - fixed)) % max(1, count - fixed)
        return jnp.zeros((count,), jnp.int32).at[sequence[jnp.where(places < fixed, places, moved)]].set(jnp.asarray(tallies, jnp.int32))

    tallies = jnp.where(number % 4 == 0, named(packed, number // 4), named(ordinary, number - number // 4 - 1))
    mixed = jax.random.permutation(jax.random.fold_in(own, 3), count)
    donor, receiver = mixed[0:count // 2 * 2:2], mixed[1:count // 2 * 2:2]
    room = jnp.minimum(tallies[donor] - 1, most - tallies[receiver]) // 2
    room = jnp.where((donor == sequence[0]) | (receiver == sequence[0]) | (tallies[receiver] == 0), 0, jnp.maximum(room, 0))
    moved = jax.random.randint(jax.random.fold_in(own, 4), (count // 2,), 0, 1 << 20) % (room + 1)
    tallies = tallies.at[donor].add(-moved).at[receiver].add(moved)
    members = jnp.searchsorted(jnp.cumsum(tallies), jnp.arange(rows * top), side="right").astype(jnp.int32)
    table = members.reshape(top, rows).T
    table = table[jax.random.permutation(jax.random.fold_in(own, 1), rows)]
    rotation = jax.random.randint(jax.random.fold_in(own, 2), (rows, 1), 0, top)
    return jnp.take_along_axis(table, (jnp.arange(top)[None, :] + rotation) % top, axis=1)


def shares(count, total, reach, lean, full):
    portions = [(1 << 20) // math.isqrt(grade ** lean) + 1 for grade in range(1, count + 1)]
    largest = reach if full else min(reach, max(-(-total // count), total * portions[0] // sum(portions)))
    least = 1 if total - largest >= count - 1 else 0
    given, spare = [largest] + [least] * (count - 1), total - largest - least * (count - 1)
    while spare > 0:
        candidates = [i for i in range(1, count) if given[i] < largest] or [i for i in range(1, count) if given[i] < reach]
        whole, budget = sum([portions[i] for i in candidates]), spare
        for i in candidates:
            more = min(reach - given[i], max(1, budget * portions[i] // whole), spare)
            given[i] = given[i] + more
            spare = spare - more
    return np.array(given)


def centred(own_key, dims, spread, limit, cuts=(), dtype=jnp.bfloat16):
    values = jax.random.normal(own_key, dims, jnp.float32) * spread
    if len(cuts) > 0:
        values = block_scale(own_key, dims, cuts, -0.22, 0.18) * values
    return jnp.clip(values, min=-limit, max=limit).astype(dtype)


def setup_inputs(seed: int = 0) -> dict:
    key_of = jax.random.split(jax.random.key(seed), 11)
    queries = draw_queries(jax.random.fold_in(key_of[10], 71), 0)
    cached_keys = draw_cached_keys(jax.random.fold_in(key_of[10], 71), 0)
    cached_values = centred(key_of[2], (REQUEST_TOTAL, CACHE_SLOTS, KEY_VALUE_HEADS * HEAD_WIDTH), 1.0, 6.0, ((0, 128),))
    lengths = draw_lengths(jax.random.fold_in(key_of[10], 71), 0)
    norm_gain = jnp.clip(1.0 + 0.15 * jax.random.normal(key_of[4], (MODEL_WIDTH,), jnp.float32), 0.25, 1.75)
    expert_ids_keys = jax.random.split(jax.random.fold_in(key_of[5], 1), REQUEST_TOTAL // DEVICE_REQUESTS)
    expert_ids_turns = jax.random.permutation(jax.random.fold_in(key_of[5], 3), REQUEST_TOTAL // DEVICE_REQUESTS)
    expert_ids = jax.vmap(lambda own, number: deal_out(jax.random.fold_in(key_of[5], 2), own, number, DEVICE_REQUESTS, EXPERTS, 2, MOST, 2))(expert_ids_keys, expert_ids_turns).reshape((REQUEST_TOTAL, 2))
    gates = jnp.clip(0.1 + 0.9 * jax.random.uniform(key_of[6], (REQUEST_TOTAL, 2), jnp.float32) ** block_scale(key_of[6], (REQUEST_TOTAL, 2), ((0, 128),), -0.2, 0.2), 0.1, 1.0)
    gate_proj = centred(key_of[7], (EXPERTS, MODEL_WIDTH, FF), MODEL_WIDTH ** -0.5, 0.109375, ((0, 8), (2, 16)))
    up_proj = centred(key_of[8], (EXPERTS, MODEL_WIDTH, FF), MODEL_WIDTH ** -0.5, 0.109375, ((0, 8), (2, 16)))
    down_proj = centred(key_of[9], (EXPERTS, FF, MODEL_WIDTH), FF ** -0.5, 0.0625, ((0, 8), (1, 16)))
    return dict(queries=queries, cached_keys=cached_keys, cached_values=cached_values, lengths=lengths, norm_gain=norm_gain, expert_ids=expert_ids, gates=gates, gate_proj=gate_proj, up_proj=up_proj, down_proj=down_proj)


def block_attention(blocks):
    block_queries, block_keys, block_values, length_block = blocks
    count_of_rows = block_queries.shape[0]
    heads_of_queries = block_queries.astype(jnp.float32).reshape(count_of_rows, KEY_VALUE_HEADS, QUERY_HEADS // KEY_VALUE_HEADS, HEAD_WIDTH)
    heads_of_keys = block_keys.astype(jnp.float32).reshape(count_of_rows, CACHE_SLOTS, KEY_VALUE_HEADS, HEAD_WIDTH)
    heads_of_values = block_values.astype(jnp.float32).reshape(count_of_rows, CACHE_SLOTS, KEY_VALUE_HEADS, HEAD_WIDTH)
    scores = jnp.einsum('rjgd,rcjd->rjgc', heads_of_queries, heads_of_keys) / math.sqrt(HEAD_WIDTH)
    valid = jnp.arange(CACHE_SLOTS)[None, :] < length_block[:, None]
    scores = jnp.where(valid[:, None, None, :], scores, -jnp.inf)
    score_peak = lax.optimization_barrier(jnp.max(scores, axis=-1, keepdims=True))
    raised = jnp.exp(scores - score_peak)
    weights = (raised / lax.optimization_barrier(jnp.sum(raised, axis=-1, keepdims=True))).astype(jnp.bfloat16)
    context_mixed = jnp.einsum('rjgc,rcjd->rjgd', weights.astype(jnp.float32), heads_of_values)
    return context_mixed.reshape(count_of_rows, MODEL_WIDTH)

def slot_table(ids_block):
    expert_hit = jnp.any(ids_block[:, :, None] == jnp.arange(EXPERTS)[None, None, :], axis=1).astype(jnp.int32)
    slot_rank = jnp.cumsum(expert_hit, axis=0) - expert_hit
    placed = (expert_hit[:, :, None] == 1) & (slot_rank[:, :, None] == jnp.arange(MOST)[None, None, :])
    return placed.astype(jnp.float32)

def mix_table(ids_block, gates_block):
    chosen = (ids_block[:, :, None] == jnp.arange(EXPERTS)[None, None, :]).astype(jnp.float32)
    per_expert = jnp.einsum('rk,rke->re', gates_block, chosen, precision=lax.Precision.HIGHEST)
    return per_expert[:, :, None] * slot_table(ids_block)

def reference(queries, cached_keys, cached_values, lengths, norm_gain, expert_ids, gates, gate_proj, up_proj, down_proj):
    every_block = N_GRP * N_TP
    context_mixed = lax.map(block_attention, (queries.reshape(every_block, DEVICE_REQUESTS, MODEL_WIDTH), cached_keys.reshape(every_block, DEVICE_REQUESTS, CACHE_SLOTS, KEY_VALUE_HEADS * HEAD_WIDTH), cached_values.reshape(every_block, DEVICE_REQUESTS, CACHE_SLOTS, KEY_VALUE_HEADS * HEAD_WIDTH), lengths.reshape(every_block, DEVICE_REQUESTS)))
    mean_square = lax.optimization_barrier(jnp.mean(context_mixed * context_mixed, axis=-1, keepdims=True))
    expert_in = (context_mixed * lax.rsqrt(mean_square + 1e-05) * norm_gain).astype(jnp.bfloat16)
    ids_blocks = expert_ids.reshape(every_block, DEVICE_REQUESTS, 2)
    gates_blocks = gates.reshape(every_block, DEVICE_REQUESTS, 2)
    tables = jax.vmap(slot_table)(ids_blocks)
    buffers = jnp.einsum('ares,ard->aesd', tables, expert_in.astype(jnp.float32))
    width = FF // N_TP
    outputs = []
    for expert in range(EXPERTS):
        tok_rows = buffers[:, expert].reshape(every_block * MOST, MODEL_WIDTH).astype(jnp.bfloat16)
        total = jnp.zeros((every_block * MOST, MODEL_WIDTH), jnp.float32)
        for shard in range(N_TP):
            low = shard * width
            gate_part = jnp.dot(tok_rows, gate_proj[expert, :, low:low + width], preferred_element_type=jnp.float32)
            up_part = jnp.dot(tok_rows, up_proj[expert, :, low:low + width], preferred_element_type=jnp.float32)
            hidden = (jax.nn.silu(gate_part) * up_part).astype(jnp.bfloat16)
            partial_out = jnp.dot(hidden, down_proj[expert, low:low + width, :], preferred_element_type=jnp.float32).astype(jnp.bfloat16)
            total = total + lax.optimization_barrier(partial_out).astype(jnp.float32)
        outputs.append(total.astype(jnp.bfloat16).reshape(every_block, MOST, MODEL_WIDTH))
    expert_out = jnp.stack(outputs, axis=1)
    mixes = jax.vmap(mix_table)(ids_blocks, gates_blocks)
    mixed = jnp.einsum('ares,aesd->ard', mixes, expert_out.astype(jnp.float32), precision=lax.Precision.HIGHEST)
    return mixed.reshape(REQUEST_TOTAL, MODEL_WIDTH).astype(jnp.bfloat16)
```

```python
import functools
import math

import jax
import jax.numpy as jnp
from jax import lax
from jax.experimental import pallas as pl
from jax.experimental.pallas import tpu as pltpu
from jax.sharding import PartitionSpec as P

HEAD_WIDTH = 128
QUERY_HEADS = 24
KEY_VALUE_HEADS = 4
MODEL_WIDTH = 3072
REQUESTS = 16
POSITIONS = 128
WIDE = 512
QUARTER = 768
HALF = 1536
EIGHTH = 384
ROWS = 16
OFFSETS = (0, 1, -1, 2, -2, 3, -3, 4)
MESH = pl.DeviceIdType.MESH
F32 = jnp.float32
BF16 = jnp.bfloat16


def iota(shape, axis):
    return lax.broadcasted_iota(jnp.int32, shape, axis)


def one_hot(mask):
    return jnp.where(mask, 1.0, 0.0).astype(BF16)


def dot(a, b):
    return jnp.dot(a, b, preferred_element_type=F32)


def offset_of(index):
    step = (index + 1) // 2
    return jnp.where(index % 2 == 1, step, -step)


def kernel(
    q_ref, k_hbm, v_hbm, len_ref, gain_ref, ids_ref, gates_ref, wg_hbm, wu_hbm, wd_hbm,
    out_ref,
    k_buf, v_buf, wg, wu, wd, q_rows, s_rows, c_rows,
    packed, landed, xs, hidden, parts, r1, r2, r3, r4, r5, r6, back, home,
    kv_sem, w_sem, z_send, z_recv, ag_send, ag_recv, rs_send, rs_recv, ret_send, ret_recv,
):
    role = lax.axis_index("role")
    z = lax.axis_index("grp")
    t = lax.axis_index("tp")
    x, y = t % 4, t // 4
    turn = 1 - 2 * role

    def at_x(step):
        return (role, z, y * 4 + (x + step * turn + 4) % 4)

    def at_y(step):
        return (role, z, ((y + step * turn + 4) % 4) * 4 + x)

    def at_z(step, core):
        return (core, (z + step + 8) % 8, t)

    near = {"x": at_x, "y": at_y}

    loads = []
    for i in range(4):
        rows = pl.ds(4 * i, 4)
        loads.append((
            pltpu.make_async_copy(k_hbm.at[rows], k_buf.at[rows], kv_sem.at[i]),
            pltpu.make_async_copy(v_hbm.at[rows], v_buf.at[rows], kv_sem.at[4 + i]),
        ))
    for kc, _ in loads:
        kc.start()
    for _, vc in loads:
        vc.start()
    weight_loads = [
        pltpu.make_async_copy(src.at[0], dst, w_sem.at[i])
        for i, (src, dst) in enumerate(((wg_hbm, wg), (wu_hbm, wu), (wd_hbm, wd)))
    ]
    for wc in weight_loads:
        wc.start()

    barrier = pltpu.get_barrier_semaphore()
    partners = [at_x(1), at_x(-1), at_y(1), at_y(-1), at_z(0, 1 - role)]
    for step in OFFSETS[1:]:
        partners += [at_z(step, role), at_z(step, 1 - role)]
    for partner in partners:
        pl.semaphore_signal(barrier, inc=1, device_id=partner, device_id_type=MESH)

    for h in range(QUERY_HEADS):
        q_rows[pl.ds(h, REQUESTS, stride=QUERY_HEADS), :] = q_ref[
            :, h * HEAD_WIDTH : (h + 1) * HEAD_WIDTH
        ].astype(F32)
    group = iota((QUERY_HEADS, HEAD_WIDTH), 0) // (QUERY_HEADS // KEY_VALUE_HEADS)
    place = iota((QUERY_HEADS, POSITIONS), 1)
    scale = 1.0 / math.sqrt(HEAD_WIDTH)
    for r in range(REQUESTS):
        if r % 4 == 0:
            loads[r // 4][0].wait()
        own = q_rows[r * QUERY_HEADS : (r + 1) * QUERY_HEADS, :]
        spread = jnp.concatenate(
            [jnp.where(group == j, own, 0.0) for j in range(KEY_VALUE_HEADS)], axis=1
        ).astype(BF16)
        scores = lax.dot_general(
            spread, k_buf[r], (((1,), (1,)), ((), ())), preferred_element_type=F32
        )
        s_rows[r * QUERY_HEADS : (r + 1) * QUERY_HEADS, :] = jnp.where(
            place < len_ref[r], scores * scale, -jnp.inf
        )
    scores = s_rows[...]
    raised = jnp.exp(scores - jnp.max(scores, axis=1, keepdims=True))
    s_rows[...] = raised / jnp.sum(raised, axis=1, keepdims=True)
    for r in range(REQUESTS):
        if r % 4 == 0:
            loads[r // 4][1].wait()
        weights = s_rows[r * QUERY_HEADS : (r + 1) * QUERY_HEADS, :].astype(BF16)
        mixed = dot(weights, v_buf[r])
        own = jnp.where(group == 0, mixed[:, :HEAD_WIDTH], 0.0)
        for j in range(1, KEY_VALUE_HEADS):
            own = jnp.where(group == j, mixed[:, j * HEAD_WIDTH : (j + 1) * HEAD_WIDTH], own)
        c_rows[r * QUERY_HEADS : (r + 1) * QUERY_HEADS, :] = own
    heads = [
        c_rows[pl.ds(h, REQUESTS, stride=QUERY_HEADS), :] for h in range(QUERY_HEADS)
    ]
    squares = heads[0] * heads[0]
    for head in heads[1:]:
        squares = squares + head * head
    mean_square = jnp.sum(squares, axis=1, keepdims=True) / MODEL_WIDTH
    norm = lax.rsqrt(mean_square + 1e-05)
    expert_in = [
        head * norm * gain_ref[:, h * HEAD_WIDTH : (h + 1) * HEAD_WIDTH]
        for h, head in enumerate(heads)
    ]
    stacked = jnp.concatenate(
        [jnp.concatenate(expert_in[6 * i : 6 * i + 6], axis=1) for i in range(4)], axis=0
    ).astype(BF16)

    diagonal = iota((16, 16), 0) == iota((16, 16), 1)
    first = jnp.sum(jnp.where(diagonal, ids_ref[:, 0:1], 0), axis=0, keepdims=True)
    second = jnp.sum(jnp.where(diagonal, ids_ref[:, 1:2], 0), axis=0, keepdims=True)
    first = jnp.concatenate([first] * 4, axis=1)
    second = jnp.concatenate([second] * 4, axis=1)
    row, col = iota((128, 64), 0), iota((128, 64), 1)
    expert = (z + offset_of(row // 16) + 8) % 8
    hit = (first == expert) | (second == expert)
    trow, tcol = iota((64, 64), 0), iota((64, 64), 1)
    earlier = (trow // 16 == tcol // 16) & (trow % 16 < tcol % 16)
    rank = dot(one_hot(hit), one_hot(earlier))
    slot = ((row // 4) % 4 + 4 * role).astype(F32)
    chosen = one_hot(hit & (rank == slot) & (row % 4 == col // 16))
    packets = dot(chosen, stacked).astype(BF16)
    packed[...] = packets.reshape(8, ROWS, QUARTER)

    pl.semaphore_wait(barrier, len(partners))

    z_copies = {}
    for j in range(1, 8):
        z_copies[j] = pltpu.make_async_remote_copy(
            src_ref=packed.at[j], dst_ref=landed.at[j],
            send_sem=z_send.at[j], recv_sem=z_recv.at[j],
            device_id=at_z(OFFSETS[j], role), device_id_type=MESH,
        )
        z_copies[j].start()
    landed[0] = packets[:ROWS]

    def spot(part, u, v):
        return v, 4 * part + u

    def chunk(ref, part, u, v):
        block, place = spot(part, u, v)
        return ref.at[block, pl.ds(place * ROWS, ROWS), :]

    axes = (("x", "y"), ("y", "x"))
    gathers = {}

    def send_chunk(part, axis, step, src, dst):
        number = part * 16 + dst[0] * 4 + dst[1]
        copy = pltpu.make_async_remote_copy(
            src_ref=chunk(xs, part, *src), dst_ref=chunk(xs, part, *dst),
            send_sem=ag_send.at[number], recv_sem=ag_recv.at[number],
            device_id=near[axes[part][axis]](step), device_id_type=MESH,
        )
        copy.start()
        gathers[part, dst[0], dst[1]] = copy

    pick_row, pick_col = iota((ROWS, 64), 0), iota((ROWS, 64), 1)
    for part in range(2):
        for j in range(4 * part, 4 * part + 4):
            if j > 0:
                z_copies[j].wait_recv()
        rows = landed[4 * part : 4 * part + 4].reshape(64, QUARTER)
        for i in range(4):
            pick = one_hot((pick_col // 4 == pick_row) & (pick_col % 4 == i))
            xs[0, 64 * part : 64 * part + ROWS, i * QUARTER : (i + 1) * QUARTER] = dot(
                pick, rows
            ).astype(BF16)
        send_chunk(part, 0, 1, (0, 0), (1, 0))
        send_chunk(part, 0, -1, (0, 0), (3, 0))
        send_chunk(part, 1, 1, (0, 0), (0, 1))
        send_chunk(part, 1, -1, (0, 0), (0, 3))

    for part in range(2):
        gathers[part, 1, 0].wait_recv()
        send_chunk(part, 0, 1, (1, 0), (2, 0))
        send_chunk(part, 1, 1, (1, 0), (1, 1))
        send_chunk(part, 1, -1, (1, 0), (1, 3))
    for part in range(2):
        gathers[part, 3, 0].wait_recv()
        send_chunk(part, 1, 1, (3, 0), (3, 1))
        send_chunk(part, 1, -1, (3, 0), (3, 3))
    for part in range(2):
        gathers[part, 0, 1].wait_recv()
        send_chunk(part, 1, 1, (0, 1), (0, 2))
    for part in range(2):
        gathers[part, 2, 0].wait_recv()
        send_chunk(part, 1, 1, (2, 0), (2, 1))
        send_chunk(part, 1, -1, (2, 0), (2, 3))

    def pass_on(u):
        for part in range(2):
            gathers[part, u, 1].wait_recv()
            send_chunk(part, 1, 1, (u, 1), (u, 2))

    def gate_up(block, i):
        cols = slice(i * 256, (i + 1) * 256)
        rows = xs[block]
        gate = dot(rows, wg[:, cols])
        up = dot(rows, wu[:, cols])
        hidden[:, cols] = (gate / (1.0 + jnp.exp(-gate)) * up).astype(BF16)

    def down(block, low, high):
        for i in range(low, high):
            cols = slice(i * 512, (i + 1) * 512)
            parts[block, :, cols] = dot(hidden[...], wd[:, cols]).astype(BF16)

    for wc in weight_loads:
        wc.wait()
    gate_up(0, 0)
    pass_on(1)
    gate_up(0, 1)
    pass_on(3)
    down(0, 0, 6)
    pass_on(2)

    def ready(v):
        for part in range(2):
            for u in range(4):
                gathers[part, u, v].wait_recv()

    sums = {}

    def send_sum(buf, base, part, u, axis, step, src):
        number = base + (part * 4 + u if base < 24 else part)
        dst = buf.at[part, u] if base < 24 else buf.at[part]
        copy = pltpu.make_async_remote_copy(
            src_ref=src, dst_ref=dst,
            send_sem=rs_send.at[number], recv_sem=rs_recv.at[number],
            device_id=near[axes[part][axis]](step), device_id_type=MESH,
        )
        copy.start()
        sums[base, part, u] = copy

    order = (2, 1, 3, 0)
    for part in range(2):
        for u in range(4):
            gathers[part, u, 3].wait_recv()
    gate_up(3, 0)
    gate_up(3, 1)
    down(3, 0, 6)
    for u in order:
        for part in range(2):
            send_sum(r2, 0, part, u, 1, 1, chunk(parts, part, u, 3))
    gate_up(1, 0)
    gate_up(1, 1)
    down(1, 0, 6)
    ready(2)
    gate_up(2, 0)
    gate_up(2, 1)
    down(2, 0, 6)
    for u in order:
        for part in range(2):
            send_sum(r1, 8, part, u, 1, -1, chunk(parts, part, u, 2))
    for u in order:
        for part in range(2):
            sums[8, part, u].wait_recv()
            mine = chunk(parts, part, u, 1)
            mine[...] = (mine[...].astype(F32) + r1[part, u].astype(F32)).astype(BF16)
            send_sum(r3, 16, part, u, 1, -1, mine)
    for u in order:
        for part in range(2):
            sums[0, part, u].wait_recv()
            sums[16, part, u].wait_recv()
            mine = chunk(parts, part, u, 0)
            mine[...] = (
                mine[...].astype(F32) + r2[part, u].astype(F32) + r3[part, u].astype(F32)
            ).astype(BF16)
            if u == 2:
                send_sum(r4, 24, part, u, 0, -1, mine)
            if u == 3:
                send_sum(r5, 26, part, u, 0, 1, mine)
    for part in range(2):
        sums[24, part, 2].wait_recv()
        mine = chunk(parts, part, 1, 0)
        mine[...] = (mine[...].astype(F32) + r4[part].astype(F32)).astype(BF16)
        send_sum(r6, 28, part, 1, 0, -1, mine)

    returns = []
    spread_row, spread_col = iota((64, ROWS), 0), iota((64, ROWS), 1)
    for part in range(2):
        sums[26, part, 3].wait_recv()
        sums[28, part, 1].wait_recv()
        total = (
            chunk(parts, part, 0, 0)[...].astype(F32)
            + r5[part].astype(F32)
            + r6[part].astype(F32)
        ).astype(BF16)
        for half in range(2):
            rows = None
            for i in range(4):
                pick = one_hot((spread_row // 4 == spread_col) & (spread_row % 4 == i))
                low = half * HALF + i * EIGHTH
                term = dot(pick, total[:, low : low + EIGHTH])
                rows = term if rows is None else rows + term
            back[half, 4 * part : 4 * part + 4] = rows.astype(BF16).reshape(4, ROWS, EIGHTH)
        for j in range(4 * part, 4 * part + 4):
            for other in range(2):
                half = role if other == 0 else 1 - role
                if j == 0 and other == 0:
                    continue
                number = j * 2 + other
                copy = pltpu.make_async_remote_copy(
                    src_ref=back.at[half, j], dst_ref=home.at[j, role],
                    send_sem=ret_send.at[number], recv_sem=ret_recv.at[number],
                    device_id=at_z(-OFFSETS[j], half), device_id_type=MESH,
                )
                copy.start()
                returns.append(copy)
        if part == 0:
            home[0, role] = back[role, 0]

    row, col = iota((REQUESTS, 256), 0), iota((REQUESTS, 256), 1)
    expert = (z + offset_of(col // 32) + 8) % 8
    hits = [ids_ref[:, k : k + 1] == expert for k in range(2)]
    earlier = one_hot(iota((16, 16), 1) < iota((16, 16), 0))
    rank = dot(earlier, one_hot(hits[0] | hits[1]))
    fits = rank == ((col // 4) % 8).astype(F32)
    for copy in returns:
        copy.wait_recv()
    rows = home[...].reshape(256, EIGHTH)
    for i in range(4):
        terms = [
            dot(one_hot(hits[k] & fits & (col % 4 == i)), rows) * gates_ref[:, k : k + 1]
            for k in range(2)
        ]
        out_ref[:, i * EIGHTH : (i + 1) * EIGHTH] = (terms[0] + terms[1]).astype(BF16)

    for copy in z_copies.values():
        copy.wait_send()
    for copy in gathers.values():
        copy.wait_send()
    for copy in sums.values():
        copy.wait_send()
    for copy in returns:
        copy.wait_send()


def local(
    queries, cached_keys, cached_values, lengths, norm_gain,
    expert_ids, gates, gate_proj, up_proj, down_proj,
):
    vmem = pl.BlockSpec(memory_space=pltpu.VMEM)
    smem = pl.BlockSpec(memory_space=pltpu.SMEM)
    hbm = pl.BlockSpec(memory_space=pl.ANY)
    dma = pltpu.SemaphoreType.DMA
    return pl.pallas_call(
        kernel,
        out_shape=jax.ShapeDtypeStruct((REQUESTS, HALF), BF16),
        in_specs=[vmem, hbm, hbm, smem, vmem, vmem, vmem, hbm, hbm, hbm],
        out_specs=vmem,
        scratch_shapes=[
            pltpu.VMEM((REQUESTS, POSITIONS, WIDE), BF16),
            pltpu.VMEM((REQUESTS, POSITIONS, WIDE), BF16),
            pltpu.VMEM((MODEL_WIDTH, WIDE), BF16),
            pltpu.VMEM((MODEL_WIDTH, WIDE), BF16),
            pltpu.VMEM((WIDE, MODEL_WIDTH), BF16),
            pltpu.VMEM((REQUESTS * QUERY_HEADS, HEAD_WIDTH), F32),
            pltpu.VMEM((REQUESTS * QUERY_HEADS, HEAD_WIDTH), F32),
            pltpu.VMEM((REQUESTS * QUERY_HEADS, HEAD_WIDTH), F32),
            pltpu.VMEM((8, ROWS, QUARTER), BF16),
            pltpu.VMEM((8, ROWS, QUARTER), BF16),
            pltpu.VMEM((4, 128, MODEL_WIDTH), BF16),
            pltpu.VMEM((128, WIDE), BF16),
            pltpu.VMEM((4, 128, MODEL_WIDTH), BF16),
            pltpu.VMEM((2, 4, ROWS, MODEL_WIDTH), BF16),
            pltpu.VMEM((2, 4, ROWS, MODEL_WIDTH), BF16),
            pltpu.VMEM((2, 4, ROWS, MODEL_WIDTH), BF16),
            pltpu.VMEM((2, ROWS, MODEL_WIDTH), BF16),
            pltpu.VMEM((2, ROWS, MODEL_WIDTH), BF16),
            pltpu.VMEM((2, ROWS, MODEL_WIDTH), BF16),
            pltpu.VMEM((2, 8, ROWS, EIGHTH), BF16),
            pltpu.VMEM((8, 2, ROWS, EIGHTH), BF16),
            dma((8,)), dma((3,)), dma((8,)), dma((8,)), dma((32,)), dma((32,)),
            dma((30,)), dma((30,)), dma((16,)), dma((16,)),
        ],
        compiler_params=pltpu.CompilerParams(
            collective_id=0, has_side_effects=True, vmem_limit_bytes=56 * 1024 * 1024
        ),
        cost_estimate=pl.CostEstimate(
            flops=5_000_000_000, bytes_accessed=14_000_000, transcendentals=400_000
        ),
    )(
        queries, cached_keys, cached_values, lengths, norm_gain.reshape(1, MODEL_WIDTH),
        expert_ids, gates, gate_proj, up_proj, down_proj,
    )


def solution(mesh):
    placed = (
        P(("grp", "tp"), None),
        P(("grp", "tp"), None, None),
        P(("grp", "tp"), None, None),
        P(("grp", "tp")),
        P(),
        P(("grp", "tp"), None),
        P(("grp", "tp"), None),
        P("grp", None, "tp"),
        P("grp", None, "tp"),
        P("grp", "tp", None),
    )
    return jax.shard_map(
        local, mesh=mesh, in_specs=placed, out_specs=P(("grp", "tp"), "role"), check_vma=False
    )
```

```python
import functools
import math

import jax
import jax.numpy as jnp
from jax import lax
from jax.experimental import pallas as pl
from jax.experimental.pallas import tpu as pltpu
from jax.sharding import PartitionSpec as P

HEAD_WIDTH = 128
QUERY_HEADS = 24
KEY_VALUE_HEADS = 4
MODEL_WIDTH = 3072
REQUESTS = 16
POSITIONS = 128
WIDE = 512
QUARTER = 768
HALF = 1536
EIGHTH = 384
ROWS = 16
OFFSETS = (0, 1, -1, 2, -2, 3, -3, 4)
PIECES = 1
MIX = (1, 0)
SPAN = 3072
FIRST_BLOCK = 0
ORDER = (
    ("unpack", 0), ("own", 0, 0, 0, 1), ("own", 0, 0, 0, -1), ("own", 0, 0, 1, 1),
    ("own", 0, 0, 1, -1), ("far", 0, 0), ("unpack", 1), ("own", 1, 0, 0, 1), ("own", 1, 0, 0, -1),
    ("own", 1, 0, 1, 1), ("own", 1, 0, 1, -1), ("far", 1, 0), ("across", 0, 0, 1, 1),
    ("across", 0, 0, 1, -1), ("across", 1, 0, 1, 1), ("across", 1, 0, 1, -1),
    ("across", 0, 0, 3, 1), ("across", 0, 0, 3, -1), ("across", 1, 0, 3, 1),
    ("across", 1, 0, 3, -1), ("pass", 0, 0, 0), ("pass", 1, 0, 0), ("across", 0, 0, 2, 1),
    ("across", 0, 0, 2, -1), ("across", 1, 0, 2, 1), ("across", 1, 0, 2, -1), ("experts", 0, 0),
    ("pass", 0, 0, 1), ("pass", 1, 0, 1), ("pass", 0, 0, 3), ("pass", 1, 0, 3), ("pass", 0, 0, 2),
    ("pass", 1, 0, 2), ("experts", 0, 3), ("direct", 1, 0, 2), ("direct", 0, 0, 2),
    ("direct", 1, 0, 1), ("direct", 0, 0, 1), ("direct", 1, 0, 3), ("direct", 0, 0, 3),
    ("direct", 1, 0, 0), ("direct", 0, 0, 0), ("experts", 0, 1), ("experts", 0, 2),
    ("opposite", 1, 0, 2), ("opposite", 0, 0, 2), ("opposite", 1, 0, 1), ("opposite", 0, 0, 1),
    ("opposite", 1, 0, 3), ("opposite", 0, 0, 3), ("opposite", 1, 0, 0), ("opposite", 0, 0, 0),
    ("sum", 1, 0, 2), ("sum", 0, 0, 2), ("sum", 1, 0, 1), ("sum", 0, 0, 1), ("sum", 1, 0, 3),
    ("sum", 0, 0, 3), ("sum", 1, 0, 0), ("sum", 0, 0, 0), ("line", 1, 0, 2), ("line", 0, 0, 2),
    ("line", 1, 0, 1), ("line", 0, 0, 1), ("line", 1, 0, 3), ("line", 0, 0, 3), ("line", 1, 0, 0),
    ("line", 0, 0, 0), ("give", 1, 0), ("give", 0, 0),
)
MESH = pl.DeviceIdType.MESH
F32 = jnp.float32
BF16 = jnp.bfloat16


def iota(shape, axis):
    return lax.broadcasted_iota(jnp.int32, shape, axis)


def one_hot(mask):
    return jnp.where(mask, 1.0, 0.0).astype(BF16)


def dot(a, b):
    return jnp.dot(a, b, preferred_element_type=F32)


def offset_of(index):
    step = (index + 1) // 2
    return jnp.where(index % 2 == 1, step, -step)


def kernel(
    q_hbm, k_hbm, v_hbm, len_ref, gain_hbm, ids_hbm, gates_hbm, wg_hbm, wu_hbm, wd_hbm,
    out_ref,
    q_buf, gain, ids, gates, k_buf, v_buf, wg, wu, wd, q_rows, s_rows, c_rows,
    packed, landed, xs, hidden, parts, r1, r2, r3, r4, r5, r6, back, home, table,
    small_sem, kv_sem, w_sem, z_send, z_recv, ag_send, ag_recv, rs_send, rs_recv,
    ret_send, ret_recv,
):
    role = lax.axis_index("role")
    z = lax.axis_index("grp")
    t = lax.axis_index("tp")
    x, y = t % 4, t // 4
    turn = 1 - 2 * role

    def at(w, axis, step):
        along_x = int(axis == w)
        col = (x + step * turn * along_x + 4) % 4
        row = (y + step * turn * (1 - along_x) + 4) % 4
        return (role, z, row * 4 + col)

    def at_z(step, core):
        return (core, (z + step + 8) % 8, t)

    barrier = pltpu.get_barrier_semaphore()
    partners = [at(0, a, step) for a in (0, 1) for step in (1, -1, 2)] + [at_z(0, 1 - role)]
    for step in OFFSETS[1:]:
        partners += [at_z(step, role), at_z(step, 1 - role)]
    for partner in partners:
        pl.semaphore_signal(barrier, inc=1, device_id=partner, device_id_type=MESH)

    small = [
        pltpu.make_async_copy(src, dst, small_sem.at[i])
        for i, (src, dst) in enumerate(
            ((q_hbm, q_buf), (ids_hbm, ids), (gain_hbm, gain), (gates_hbm, gates))
        )
    ]
    loads = []
    for i in range(4):
        rows = pl.ds(4 * i, 4)
        loads.append((
            pltpu.make_async_copy(k_hbm.at[rows], k_buf.at[rows], kv_sem.at[i]),
            pltpu.make_async_copy(v_hbm.at[rows], v_buf.at[rows], kv_sem.at[4 + i]),
        ))
    weight_loads = [
        pltpu.make_async_copy(src.at[0], dst, w_sem.at[i])
        for i, (src, dst) in enumerate(((wg_hbm, wg), (wu_hbm, wu), (wd_hbm, wd)))
    ]
    small[0].start()
    for kc, _ in loads:
        kc.start()
    for _, vc in loads:
        vc.start()
    for copy in small[1:]:
        copy.start()

    small[0].wait()
    for h in range(QUERY_HEADS):
        q_rows[pl.ds(h, REQUESTS, stride=QUERY_HEADS), :] = q_buf[
            :, h * HEAD_WIDTH : (h + 1) * HEAD_WIDTH
        ].astype(F32)
    group = iota((QUERY_HEADS, HEAD_WIDTH), 0) // (QUERY_HEADS // KEY_VALUE_HEADS)
    place = iota((QUERY_HEADS, POSITIONS), 1)
    scale = 1.0 / math.sqrt(HEAD_WIDTH)
    for r in range(REQUESTS):
        if r % 4 == 0:
            loads[r // 4][0].wait()
        own = q_rows[r * QUERY_HEADS : (r + 1) * QUERY_HEADS, :]
        spread = jnp.concatenate(
            [jnp.where(group == j, own, 0.0) for j in range(KEY_VALUE_HEADS)], axis=1
        ).astype(BF16)
        scores = lax.dot_general(
            spread, k_buf[r], (((1,), (1,)), ((), ())), preferred_element_type=F32
        )
        s_rows[r * QUERY_HEADS : (r + 1) * QUERY_HEADS, :] = jnp.where(
            place < len_ref[r], scores * scale, -jnp.inf
        )
    for wc in weight_loads:
        wc.start()
    scores = s_rows[...]
    raised = jnp.exp(scores - jnp.max(scores, axis=1, keepdims=True))
    s_rows[...] = raised / jnp.sum(raised, axis=1, keepdims=True)
    for r in range(REQUESTS):
        if r % 4 == 0:
            loads[r // 4][1].wait()
        weights = s_rows[r * QUERY_HEADS : (r + 1) * QUERY_HEADS, :].astype(BF16)
        mixed = dot(weights, v_buf[r])
        own = jnp.where(group == 0, mixed[:, :HEAD_WIDTH], 0.0)
        for j in range(1, KEY_VALUE_HEADS):
            own = jnp.where(group == j, mixed[:, j * HEAD_WIDTH : (j + 1) * HEAD_WIDTH], own)
        c_rows[r * QUERY_HEADS : (r + 1) * QUERY_HEADS, :] = own
    for copy in small[1:]:
        copy.wait()
    heads = [
        c_rows[pl.ds(h, REQUESTS, stride=QUERY_HEADS), :] for h in range(QUERY_HEADS)
    ]
    squares = heads[0] * heads[0]
    for head in heads[1:]:
        squares = squares + head * head
    mean_square = jnp.sum(squares, axis=1, keepdims=True) / MODEL_WIDTH
    norm = lax.rsqrt(mean_square + 1e-05)
    expert_in = [
        head * norm * gain[:, h * HEAD_WIDTH : (h + 1) * HEAD_WIDTH]
        for h, head in enumerate(heads)
    ]
    stacked = jnp.concatenate(
        [jnp.concatenate(expert_in[6 * i : 6 * i + 6], axis=1) for i in range(4)], axis=0
    ).astype(BF16)

    diagonal = iota((16, 16), 0) == iota((16, 16), 1)
    first = jnp.concatenate([ids[0:1, :]] * 4, axis=1)
    second = jnp.concatenate([ids[1:2, :]] * 4, axis=1)
    row, col = iota((128, 64), 0), iota((128, 64), 1)
    expert = (z + turn * offset_of(row // 16) + 8) % 8
    hit = (first == expert) | (second == expert)
    trow, tcol = iota((64, 64), 0), iota((64, 64), 1)
    earlier = (trow // 16 == tcol // 16) & (trow % 16 < tcol % 16)
    rank = dot(one_hot(hit), one_hot(earlier))
    slot = ((row // 4) % 4 + 4 * role).astype(F32)
    chosen = one_hot(hit & (rank == slot) & (row % 4 == col // 16))
    packets = dot(chosen, stacked).astype(BF16)
    packed[...] = packets.reshape(8, ROWS, QUARTER)

    pl.semaphore_wait(barrier, len(partners))

    z_copies = {}
    for j in range(1, 8):
        z_copies[j] = pltpu.make_async_remote_copy(
            src_ref=packed.at[j], dst_ref=landed.at[j],
            send_sem=z_send.at[j], recv_sem=z_recv.at[j],
            device_id=at_z(turn * OFFSETS[j], role), device_id_type=MESH,
        )
        z_copies[j].start()
    landed[0] = packets[:ROWS]

    def piece(ref, w, h, u, v):
        rows = pl.ds((w * 4 + u) * ROWS, ROWS)
        return ref.at[v, rows, pl.ds(h * SPAN, SPAN)]

    copies = {}
    seen = set()

    def arrived(key):
        if key not in seen:
            seen.add(key)
            copies[key].wait_recv()

    def gather(w, h, axis, step, u, v):
        du, dv = ((u + step) % 4, v) if axis == 0 else (u, (v + step) % 4)
        number = ((w * PIECES + h) * 4 + du) * 4 + dv
        copy = pltpu.make_async_remote_copy(
            src_ref=piece(xs, w, h, u, v), dst_ref=piece(xs, w, h, du, dv),
            send_sem=ag_send.at[number], recv_sem=ag_recv.at[number],
            device_id=at(w, axis, step), device_id_type=MESH,
        )
        copy.start()
        copies["row", w, h, du, dv] = copy

    pick_row, pick_col = iota((64, 64), 0), iota((64, 64), 1)
    picks = one_hot((pick_col // 4 == pick_row % 16) & (pick_col % 4 == pick_row // 16))

    def unpack(w):
        for j in range(4 * w, 4 * w + 4):
            if j > 0:
                z_copies[j].wait_recv()
        rows = dot(picks, landed[4 * w : 4 * w + 4].reshape(64, QUARTER)).astype(BF16)
        low = 4 * w * ROWS
        for i in range(4):
            xs[0, low : low + ROWS, i * QUARTER : (i + 1) * QUARTER] = rows[
                i * ROWS : (i + 1) * ROWS
            ]

    def own(w, h, axis, step):
        gather(w, h, axis, step, 0, 0)

    def far(w, h):
        gather(w, h, 0, 2, 0, 0)

    def across(w, h, u, step):
        arrived(("row", w, h, u, 0))
        gather(w, h, 1, step, u, 0)

    def pass_on(w, h, u):
        arrived(("row", w, h, u, 1))
        gather(w, h, 1, 1, u, 1)

    def experts(_, v):
        if v == FIRST_BLOCK:
            for wc in weight_loads:
                wc.wait()
        for w in range(2):
            for h in range(PIECES):
                for u in range(4):
                    if (u, v) != (0, 0):
                        arrived(("row", w, h, u, v))
        for n in range(2):
            cols = slice(n * 256, (n + 1) * 256)
            gate = dot(xs[v], wg[:, cols])
            up = dot(xs[v], wu[:, cols])
            hidden[:, cols] = (gate / (1.0 + jnp.exp(-gate)) * up).astype(BF16)
        for n in range(6):
            cols = slice(n * 512, (n + 1) * 512)
            parts[v, :, cols] = dot(hidden[...], wd[:, cols]).astype(BF16)

    def send_sum(kind, w, h, u, axis, step, src):
        buf = (r1, r2, r3, r4, r5, r6)[kind - 1]
        cols = pl.ds(h * SPAN, SPAN)
        if kind <= 3:
            dst, number = buf.at[w, u, :, cols], ((kind * 2 - 2 + w) * 4 + u) * PIECES + h
        else:
            dst, number = buf.at[w, :, cols], (24 + (kind - 4) * 2 + w) * PIECES + h
        copy = pltpu.make_async_remote_copy(
            src_ref=src, dst_ref=dst,
            send_sem=rs_send.at[number], recv_sem=rs_recv.at[number],
            device_id=at(w, axis, step), device_id_type=MESH,
        )
        copy.start()
        copies[kind, w, h, u if kind <= 3 else 0] = copy

    def landing(kind, w, h, u):
        arrived((kind, w, h, u))
        buf = (r1, r2, r3, r4, r5, r6)[kind - 1]
        cols = slice(h * SPAN, (h + 1) * SPAN)
        return (buf[w, u, :, cols] if kind <= 3 else buf[w, :, cols]).astype(F32)

    def sum_direct(w, h, u):
        send_sum(2, w, h, u, 1, 1, piece(parts, w, h, u, 3))

    def sum_opposite(w, h, u):
        send_sum(1, w, h, u, 1, -1, piece(parts, w, h, u, 2))

    def sum_pass(w, h, u):
        mine = piece(parts, w, h, u, 1)
        mine[...] = (mine[...].astype(F32) + landing(1, w, h, u)).astype(BF16)
        send_sum(3, w, h, u, 1, -1, mine)

    def sum_line(w, h, u):
        mine = piece(parts, w, h, u, 0)
        mine[...] = (
            mine[...].astype(F32) + landing(2, w, h, u) + landing(3, w, h, u)
        ).astype(BF16)
        if u > 0:
            send_sum(3 + u, w, h, u, 0, (-1, 2, 1)[u - 1], mine)

    returns = {}
    spreads = one_hot((pick_row // 4 == pick_col % 16) & (pick_row % 4 == pick_col // 16))

    def give_back(w, h):
        total = (
            piece(parts, w, h, 0, 0)[...].astype(F32)
            + landing(4, w, h, 0)
            + landing(5, w, h, 0)
            + landing(6, w, h, 0)
        ).astype(BF16)
        halves = range(2) if PIECES == 1 else (h,)
        for half in halves:
            low = half * HALF if PIECES == 1 else 0
            rows = jnp.concatenate(
                [total[:, low + i * EIGHTH : low + (i + 1) * EIGHTH] for i in range(4)], axis=0
            )
            rows = dot(spreads, rows)
            back[half, 4 * w : 4 * w + 4] = rows.astype(BF16).reshape(4, ROWS, EIGHTH)
        for j in (3, 2, 1, 0) if w == 0 else (7, 6, 5, 4):
            for half in halves:
                number = j * 2 + half
                copy = pltpu.make_async_remote_copy(
                    src_ref=back.at[half, j], dst_ref=home.at[j, role],
                    send_sem=ret_send.at[number], recv_sem=ret_recv.at[j * 2 + role],
                    device_id=at_z(-turn * OFFSETS[j], half), device_id_type=MESH,
                )
                returns[j, half] = copy
                if j > 0:
                    copy.start()
            if j == 0 and sum(key[0] == 0 for key in returns) == 2:
                copy = pltpu.make_async_remote_copy(
                    src_ref=back.at[1 - role, 0], dst_ref=home.at[0, role],
                    send_sem=ret_send.at[0], recv_sem=ret_recv.at[0],
                    device_id=at_z(0, 1 - role), device_id_type=MESH,
                )
                copy.start()
                sibling.append(copy)
                home[0, role] = back[role, 0]

    sibling = []

    def mix_table():
        row, col = iota((128, 256), 0), iota((128, 256), 1)
        core = (col // 16) % 2
        expert = (z + (1 - 2 * core) * offset_of(col // 32) + 8) % 8
        names = [
            jnp.sum(jnp.where(diagonal, ids[k : k + 1, :], 0), axis=1, keepdims=True)
            for k in range(2)
        ]
        names = [jnp.concatenate([name] * 8, axis=0) for name in names]
        hit = (names[0] == expert) | (names[1] == expert)
        trow, tcol = iota((128, 128), 0), iota((128, 128), 1)
        before = one_hot((trow // 16 == tcol // 16) & (tcol < trow))
        rank = dot(before, one_hot(hit))
        fits = (rank == ((col // 4) % 8).astype(F32)) & (col % 4 == (row // 16) % 4)
        named = jnp.where(row < 64, names[0], names[1]) == expert
        table[...] = one_hot(named & fits)

    def mix(w, so_far):
        for j in range(4 * w, 4 * w + 4):
            for core in range(2):
                if j == 0 and core == 0:
                    sibling[0].wait_recv()
                elif j > 0:
                    pltpu.make_async_remote_copy(
                        src_ref=back.at[core, j], dst_ref=home.at[j, core],
                        send_sem=ret_send.at[j * 2 + core], recv_sem=ret_recv.at[j * 2 + core],
                        device_id=at_z(turn, role), device_id_type=MESH,
                    ).wait_recv()
        rows = home[4 * w : 4 * w + 4].reshape(128, EIGHTH)
        terms = dot(table[:, 128 * w : 128 * w + 128], rows)
        new = []
        for i in range(4):
            total = so_far[i] if so_far else 0.0
            for k in range(2):
                low = (k * 4 + i) * ROWS
                total = total + terms[low : low + ROWS] * weight[k]
            new.append(total)
        return new

    weight = [
        jnp.sum(jnp.where(diagonal, gates[k : k + 1, :], 0.0), axis=1, keepdims=True)
        for k in range(2)
    ]

    steps = {
        "unpack": unpack, "own": own, "far": far, "across": across, "pass": pass_on,
        "experts": experts, "direct": sum_direct, "opposite": sum_opposite, "sum": sum_pass,
        "line": sum_line, "give": give_back,
    }
    for name, *where in ORDER:
        if name == "give" and not returns:
            mix_table()
        steps[name](*where)
    mixed = mix(MIX[1], mix(MIX[0], None))
    for i in range(4):
        out_ref[:, i * EIGHTH : (i + 1) * EIGHTH] = mixed[i].astype(BF16)

    for copy in list(z_copies.values()) + list(copies.values()) + sibling:
        copy.wait_send()
    for (j, _), copy in returns.items():
        if j > 0:
            copy.wait_send()


def local(
    queries, cached_keys, cached_values, lengths, norm_gain,
    expert_ids, gates, gate_proj, up_proj, down_proj,
):
    vmem = pl.BlockSpec(memory_space=pltpu.VMEM)
    smem = pl.BlockSpec(memory_space=pltpu.SMEM)
    hbm = pl.BlockSpec(memory_space=pl.ANY)
    dma = pltpu.SemaphoreType.DMA
    return pl.pallas_call(
        kernel,
        out_shape=jax.ShapeDtypeStruct((REQUESTS, HALF), BF16),
        in_specs=[hbm, hbm, hbm, smem, hbm, hbm, hbm, hbm, hbm, hbm],
        out_specs=vmem,
        scratch_shapes=[
            pltpu.VMEM((REQUESTS, MODEL_WIDTH), BF16),
            pltpu.VMEM((1, MODEL_WIDTH), F32),
            pltpu.VMEM((2, REQUESTS), jnp.int32),
            pltpu.VMEM((2, REQUESTS), F32),
            pltpu.VMEM((REQUESTS, POSITIONS, WIDE), BF16),
            pltpu.VMEM((REQUESTS, POSITIONS, WIDE), BF16),
            pltpu.VMEM((MODEL_WIDTH, WIDE), BF16),
            pltpu.VMEM((MODEL_WIDTH, WIDE), BF16),
            pltpu.VMEM((WIDE, MODEL_WIDTH), BF16),
            pltpu.VMEM((REQUESTS * QUERY_HEADS, HEAD_WIDTH), F32),
            pltpu.VMEM((REQUESTS * QUERY_HEADS, HEAD_WIDTH), F32),
            pltpu.VMEM((REQUESTS * QUERY_HEADS, HEAD_WIDTH), F32),
            pltpu.VMEM((8, ROWS, QUARTER), BF16),
            pltpu.VMEM((8, ROWS, QUARTER), BF16),
            pltpu.VMEM((4, 128, MODEL_WIDTH), BF16),
            pltpu.VMEM((128, WIDE), BF16),
            pltpu.VMEM((4, 128, MODEL_WIDTH), BF16),
            pltpu.VMEM((2, 4, ROWS, MODEL_WIDTH), BF16),
            pltpu.VMEM((2, 4, ROWS, MODEL_WIDTH), BF16),
            pltpu.VMEM((2, 4, ROWS, MODEL_WIDTH), BF16),
            pltpu.VMEM((2, ROWS, MODEL_WIDTH), BF16),
            pltpu.VMEM((2, ROWS, MODEL_WIDTH), BF16),
            pltpu.VMEM((2, ROWS, MODEL_WIDTH), BF16),
            pltpu.VMEM((2, 8, ROWS, EIGHTH), BF16),
            pltpu.VMEM((8, 2, ROWS, EIGHTH), BF16),
            pltpu.VMEM((128, 256), BF16),
            dma((4,)), dma((8,)), dma((3,)), dma((8,)), dma((8,)), dma((32 * PIECES,)), dma((32 * PIECES,)),
            dma((30 * PIECES,)), dma((30 * PIECES,)), dma((16,)), dma((16,)),
        ],
        compiler_params=pltpu.CompilerParams(
            collective_id=0, has_side_effects=True, vmem_limit_bytes=56 * 1024 * 1024
        ),
        cost_estimate=pl.CostEstimate(
            flops=5_000_000_000, bytes_accessed=14_000_000, transcendentals=400_000
        ),
    )(
        queries, cached_keys, cached_values, lengths, norm_gain.reshape(1, MODEL_WIDTH),
        expert_ids.T, gates.T, gate_proj, up_proj, down_proj,
    )


def solution(mesh):
    placed = (
        P(("grp", "tp"), None),
        P(("grp", "tp"), None, None),
        P(("grp", "tp"), None, None),
        P(("grp", "tp")),
        P(),
        P(("grp", "tp"), None),
        P(("grp", "tp"), None),
        P("grp", None, "tp"),
        P("grp", None, "tp"),
        P("grp", "tp", None),
    )
    return jax.shard_map(
        local, mesh=mesh, in_specs=placed, out_specs=P(("grp", "tp"), "role"), check_vma=False
    )
```

```python
import functools
import math

import jax
import jax.numpy as jnp
from jax import lax
from jax.experimental import pallas as pl
from jax.experimental.pallas import tpu as pltpu
from jax.sharding import PartitionSpec as P

HEAD_WIDTH = 128
QUERY_HEADS = 24
KEY_VALUE_HEADS = 4
MODEL_WIDTH = 3072
REQUESTS = 16
POSITIONS = 128
WIDE = 512
QUARTER = 768
HALF = 1536
EIGHTH = 384
ROWS = 16
OFFSETS = (0, 1, -1, 2, -2, 3, -3, 4)
MIX = (1, 0)
FIRST_BLOCK = 0
ORDER = (
    ("unpack", 0), ("own", 0, 0, 1), ("own", 0, 0, -1), ("own", 0, 1, 1), ("own", 0, 1, -1),
    ("far", 0), ("unpack", 1), ("own", 1, 0, 1), ("own", 1, 0, -1), ("own", 1, 1, 1),
    ("own", 1, 1, -1), ("far", 1), ("across", 0, 1, 1), ("across", 0, 1, -1), ("across", 1, 1, 1),
    ("across", 1, 1, -1), ("across", 0, 3, 1), ("across", 0, 3, -1), ("across", 1, 3, 1),
    ("across", 1, 3, -1), ("pass", 0, 0), ("pass", 1, 0), ("across", 0, 2, 1),
    ("across", 0, 2, -1), ("across", 1, 2, 1), ("across", 1, 2, -1), ("experts", 0),
    ("pass", 0, 1), ("pass", 1, 1), ("pass", 0, 3), ("pass", 1, 3), ("pass", 0, 2),
    ("pass", 1, 2), ("experts", 3), ("direct", 1, 2), ("direct", 0, 2), ("direct", 1, 1),
    ("direct", 0, 1), ("direct", 1, 3), ("direct", 0, 3), ("direct", 1, 0), ("direct", 0, 0),
    ("experts", 1), ("experts", 2), ("opposite", 1, 2), ("opposite", 0, 2), ("opposite", 1, 1),
    ("opposite", 0, 1), ("opposite", 1, 3), ("opposite", 0, 3), ("opposite", 1, 0),
    ("opposite", 0, 0), ("sum", 1, 2), ("sum", 0, 2), ("sum", 1, 1), ("sum", 0, 1), ("sum", 1, 3),
    ("sum", 0, 3), ("sum", 1, 0), ("sum", 0, 0), ("line", 1, 2), ("line", 0, 2), ("line", 1, 1),
    ("line", 0, 1), ("line", 1, 3), ("line", 0, 3), ("line", 1, 0), ("line", 0, 0), ("give", 1),
    ("give", 0),
)
MESH = pl.DeviceIdType.MESH
F32 = jnp.float32
BF16 = jnp.bfloat16


def iota(shape, axis):
    return lax.broadcasted_iota(jnp.int32, shape, axis)


def one_hot(mask):
    return jnp.where(mask, 1.0, 0.0).astype(BF16)


def dot(a, b):
    return jnp.dot(a, b, preferred_element_type=F32)


def offset_of(index):
    step = (index + 1) // 2
    return jnp.where(index % 2 == 1, step, -step)


def kernel(
    q_hbm, k_hbm, v_hbm, len_hbm, gain_hbm, ids_hbm, gates_hbm, wg_hbm, wu_hbm, wd_hbm,
    out_ref,
    q_buf, gain, ids, gates, k_buf, v_buf, wg, wu, wd, q_rows, s_rows, c_rows,
    packed, landed, xs, hidden, parts, r1, r2, r3, back, home, table, lengths,
    local_sem, sent, z_recv, ag_recv, rs_recv, ret_recv,
):
    role = lax.axis_index("role")
    z = lax.axis_index("grp")
    t = lax.axis_index("tp")
    x, y = t % 4, t // 4
    turn = 1 - 2 * role

    def at(w, axis, step):
        along_x = int(axis == w)
        col = (x + step * turn * along_x + 4) % 4
        row = (y + step * turn * (1 - along_x) + 4) % 4
        return (role, z, row * 4 + col)

    def at_z(step, core):
        return (core, (z + step + 8) % 8, t)

    barrier = pltpu.get_barrier_semaphore()
    partners = [at(0, a, step) for a in (0, 1) for step in (1, -1, 2)] + [at_z(0, 1 - role)]
    for step in OFFSETS[1:]:
        partners += [at_z(step, role), at_z(step, 1 - role)]
    for partner in partners:
        pl.semaphore_signal(barrier, inc=1, device_id=partner, device_id_type=MESH)

    small = [
        pltpu.make_async_copy(src, dst, local_sem.at[i])
        for i, (src, dst) in enumerate(
            ((q_hbm, q_buf), (len_hbm, lengths), (ids_hbm, ids), (gain_hbm, gain),
             (gates_hbm, gates))
        )
    ]
    loads = []
    for i in range(4):
        rows = pl.ds(4 * i, 4)
        loads.append((
            pltpu.make_async_copy(k_hbm.at[rows], k_buf.at[rows], local_sem.at[8 + i]),
            pltpu.make_async_copy(v_hbm.at[rows], v_buf.at[rows], local_sem.at[12 + i]),
        ))
    weight_loads = [
        pltpu.make_async_copy(src.at[0], dst, local_sem.at[5 + i])
        for i, (src, dst) in enumerate(((wg_hbm, wg), (wu_hbm, wu), (wd_hbm, wd)))
    ]
    small[0].start()
    small[1].start()
    for kc, _ in loads:
        kc.start()
    for _, vc in loads:
        vc.start()
    for copy in small[2:]:
        copy.start()

    small[0].wait()
    for h in range(QUERY_HEADS):
        q_rows[pl.ds(h, REQUESTS, stride=QUERY_HEADS), :] = q_buf[
            :, h * HEAD_WIDTH : (h + 1) * HEAD_WIDTH
        ].astype(F32)
    small[1].wait()
    group = iota((QUERY_HEADS, HEAD_WIDTH), 0) // (QUERY_HEADS // KEY_VALUE_HEADS)
    place = iota((QUERY_HEADS, POSITIONS), 1)
    scale = 1.0 / math.sqrt(HEAD_WIDTH)
    for r in range(REQUESTS):
        if r % 4 == 0:
            loads[r // 4][0].wait()
        own = q_rows[r * QUERY_HEADS : (r + 1) * QUERY_HEADS, :]
        spread = jnp.concatenate(
            [jnp.where(group == j, own, 0.0) for j in range(KEY_VALUE_HEADS)], axis=1
        ).astype(BF16)
        scores = lax.dot_general(
            spread, k_buf[r], (((1,), (1,)), ((), ())), preferred_element_type=F32
        )
        s_rows[r * QUERY_HEADS : (r + 1) * QUERY_HEADS, :] = jnp.where(
            place < lengths[r], scores * scale, -jnp.inf
        )
    for wc in weight_loads:
        wc.start()
    scores = s_rows[...]
    raised = jnp.exp(scores - jnp.max(scores, axis=1, keepdims=True))
    s_rows[...] = raised / jnp.sum(raised, axis=1, keepdims=True)
    for r in range(REQUESTS):
        if r % 4 == 0:
            loads[r // 4][1].wait()
        weights = s_rows[r * QUERY_HEADS : (r + 1) * QUERY_HEADS, :].astype(BF16)
        mixed = dot(weights, v_buf[r])
        own = jnp.where(group == 0, mixed[:, :HEAD_WIDTH], 0.0)
        for j in range(1, KEY_VALUE_HEADS):
            own = jnp.where(group == j, mixed[:, j * HEAD_WIDTH : (j + 1) * HEAD_WIDTH], own)
        c_rows[r * QUERY_HEADS : (r + 1) * QUERY_HEADS, :] = own
    for copy in small[2:]:
        copy.wait()
    heads = [
        c_rows[pl.ds(h, REQUESTS, stride=QUERY_HEADS), :] for h in range(QUERY_HEADS)
    ]
    squares = heads[0] * heads[0]
    for head in heads[1:]:
        squares = squares + head * head
    mean_square = jnp.sum(squares, axis=1, keepdims=True) / MODEL_WIDTH
    norm = lax.rsqrt(mean_square + 1e-05)
    expert_in = [
        head * norm * gain[:, h * HEAD_WIDTH : (h + 1) * HEAD_WIDTH]
        for h, head in enumerate(heads)
    ]
    stacked = jnp.concatenate(
        [jnp.concatenate(expert_in[6 * i : 6 * i + 6], axis=1) for i in range(4)], axis=0
    ).astype(BF16)

    diagonal = iota((16, 16), 0) == iota((16, 16), 1)
    first = jnp.concatenate([ids[0:1, :]] * 4, axis=1)
    second = jnp.concatenate([ids[1:2, :]] * 4, axis=1)
    row, col = iota((128, 64), 0), iota((128, 64), 1)
    expert = (z + turn * offset_of(row // 16) + 8) % 8
    hit = (first == expert) | (second == expert)
    trow, tcol = iota((64, 64), 0), iota((64, 64), 1)
    earlier = (trow // 16 == tcol // 16) & (trow % 16 < tcol % 16)
    rank = dot(one_hot(hit), one_hot(earlier))
    slot = ((row // 4) % 4 + 4 * role).astype(F32)
    chosen = one_hot(hit & (rank == slot) & (row % 4 == col // 16))
    packets = dot(chosen, stacked).astype(BF16)
    packed[...] = packets.reshape(8, ROWS, QUARTER)

    pl.semaphore_wait(barrier, len(partners))

    def landing(ref, sem):
        pltpu.make_async_copy(ref, ref, sem).wait()

    for j in (1, 2, 3, 7, 5, 6, 4):
        pltpu.make_async_remote_copy(
            src_ref=packed.at[j], dst_ref=landed.at[j],
            send_sem=sent.at[0], recv_sem=z_recv.at[j // 4],
            device_id=at_z(turn * OFFSETS[j], role), device_id_type=MESH,
        ).start()
    landed[0] = packets[:ROWS]

    def block(ref, w, u, v):
        return ref.at[pl.ds((v * 8 + w * 4 + u) * ROWS, ROWS), :]

    def gather(w, axis, step, u, v):
        du, dv = ((u + step) % 4, v) if axis == 0 else (u, (v + step) % 4)
        number = (w * 3 + du - 1, 6 + w * 4 + du, 14, 15)[dv]
        pltpu.make_async_remote_copy(
            src_ref=block(xs, w, u, v), dst_ref=block(xs, w, du, dv),
            send_sem=sent.at[1], recv_sem=ag_recv.at[number],
            device_id=at(w, axis, step), device_id_type=MESH,
        ).start()

    seen = set()

    def arrived(w, u, v):
        if (w, u, v) not in seen:
            seen.add((w, u, v))
            landing(block(xs, w, u, v), ag_recv.at[w * 3 + u - 1 if v == 0 else 6 + w * 4 + u])

    pick_row, pick_col = iota((64, 64), 0), iota((64, 64), 1)
    picks = one_hot((pick_col // 4 == pick_row % 16) & (pick_col % 4 == pick_row // 16))

    def unpack(w):
        first = max(4 * w, 1)
        landing(landed.at[pl.ds(first, 4 * w + 4 - first)], z_recv.at[w])
        rows = dot(picks, landed[4 * w : 4 * w + 4].reshape(64, QUARTER)).astype(BF16)
        low = 4 * w * ROWS
        for i in range(4):
            xs[low : low + ROWS, i * QUARTER : (i + 1) * QUARTER] = rows[
                i * ROWS : (i + 1) * ROWS
            ]

    def own(w, axis, step):
        gather(w, axis, step, 0, 0)

    def far(w):
        gather(w, 0, 2, 0, 0)

    def across(w, u, step):
        arrived(w, u, 0)
        gather(w, 1, step, u, 0)

    def pass_on(w, u):
        arrived(w, u, 1)
        gather(w, 1, 1, u, 1)

    def experts(v):
        if v == FIRST_BLOCK:
            for wc in weight_loads:
                wc.wait()
        low = v * 128
        if v > 1:
            landing(xs.at[pl.ds(low, 128)], ag_recv.at[12 + v])
        else:
            for w in range(2):
                for u in range(1 - v, 4):
                    arrived(w, u, v)
        for n in range(2):
            cols = slice(n * 256, (n + 1) * 256)
            gate = dot(xs[low : low + 128], wg[:, cols])
            up = dot(xs[low : low + 128], wu[:, cols])
            hidden[:, cols] = (gate / (1.0 + jnp.exp(-gate)) * up).astype(BF16)
        for n in range(6):
            cols = slice(n * 512, (n + 1) * 512)
            parts[low : low + 128, cols] = dot(hidden[...], wd[:, cols]).astype(BF16)

    def send_sum(src, dst, number, w, axis, step):
        pltpu.make_async_remote_copy(
            src_ref=src, dst_ref=dst, send_sem=sent.at[2], recv_sem=rs_recv.at[number],
            device_id=at(w, axis, step), device_id_type=MESH,
        ).start()

    def sum_direct(w, u):
        send_sum(block(parts, w, u, 3), r2.at[w, u, 0], 8 + w * 4 + u, w, 1, 1)

    def sum_opposite(w, u):
        send_sum(block(parts, w, u, 2), r1.at[w, u], w * 4 + u, w, 1, -1)

    def sum_pass(w, u):
        landing(r1.at[w, u], rs_recv.at[w * 4 + u])
        mine = block(parts, w, u, 1)
        mine[...] = (mine[...].astype(F32) + r1[w, u].astype(F32)).astype(BF16)
        send_sum(mine, r2.at[w, u, 1], 8 + w * 4 + u, w, 1, -1)

    def sum_line(w, u):
        landing(r2.at[w, u], rs_recv.at[8 + w * 4 + u])
        mine = block(parts, w, u, 0)
        mine[...] = (
            mine[...].astype(F32) + r2[w, u, 0].astype(F32) + r2[w, u, 1].astype(F32)
        ).astype(BF16)
        if u > 0:
            send_sum(mine, r3.at[w, u - 1], 16 + w, w, 0, (-1, 2, 1)[u - 1])

    spreads = one_hot((pick_row // 4 == pick_col % 16) & (pick_row % 4 == pick_col // 16))

    def give_back(w):
        landing(r3.at[w], rs_recv.at[16 + w])
        total = block(parts, w, 0, 0)[...].astype(F32)
        for i in range(3):
            total = total + r3[w, i].astype(F32)
        total = total.astype(BF16)
        for half in range(2):
            cols = [half * HALF + i * EIGHTH for i in range(4)]
            rows = jnp.concatenate([total[:, low : low + EIGHTH] for low in cols], axis=0)
            low = half * 8 + 4 * w
            back[low : low + 4] = dot(spreads, rows).astype(BF16).reshape(4, ROWS, EIGHTH)
        for j in range(4 * w + 3, 4 * w - 1, -1):
            for other in range(2):
                half = role if other == 0 else 1 - role
                if j == 0 and other == 0:
                    home[0] = back[half * 8]
                    continue
                pltpu.make_async_remote_copy(
                    src_ref=back.at[half * 8 + j], dst_ref=home.at[j * 2 + other],
                    send_sem=sent.at[3], recv_sem=ret_recv.at[w],
                    device_id=at_z(-turn * OFFSETS[j], half), device_id_type=MESH,
                ).start()

    def mix_table():
        row, col = iota((128, 256), 0), iota((128, 256), 1)
        other = (col // 16) % 2
        core = role + other - 2 * role * other
        expert = (z + (1 - 2 * core) * offset_of(col // 32) + 8) % 8
        names = [
            jnp.sum(jnp.where(diagonal, ids[k : k + 1, :], 0), axis=1, keepdims=True)
            for k in range(2)
        ]
        names = [jnp.concatenate([name] * 8, axis=0) for name in names]
        hit = (names[0] == expert) | (names[1] == expert)
        trow, tcol = iota((128, 128), 0), iota((128, 128), 1)
        before = one_hot((trow // 16 == tcol // 16) & (tcol < trow))
        rank = dot(before, one_hot(hit))
        fits = (rank == (col % 16 // 4 + 4 * core).astype(F32)) & (col % 4 == (row // 16) % 4)
        named = jnp.where(row < 64, names[0], names[1]) == expert
        table[...] = one_hot(named & fits)

    def mix(w, so_far):
        first = max(8 * w, 1)
        landing(home.at[pl.ds(first, 8 * w + 8 - first)], ret_recv.at[w])
        rows = home[8 * w : 8 * w + 8].reshape(128, EIGHTH)
        terms = dot(table[:, 128 * w : 128 * w + 128], rows)
        new = []
        for i in range(4):
            total = so_far[i] if so_far else 0.0
            for k in range(2):
                low = (k * 4 + i) * ROWS
                total = total + terms[low : low + ROWS] * weight[k]
            new.append(total)
        return new

    weight = [
        jnp.sum(jnp.where(diagonal, gates[k : k + 1, :], 0.0), axis=1, keepdims=True)
        for k in range(2)
    ]

    steps = {
        "unpack": unpack, "own": own, "far": far, "across": across, "pass": pass_on,
        "experts": experts, "direct": sum_direct, "opposite": sum_opposite, "sum": sum_pass,
        "line": sum_line, "give": give_back,
    }
    mix_table()
    for name, *where in ORDER:
        steps[name](*where)
    mixed = mix(MIX[1], mix(MIX[0], None))
    for i in range(4):
        out_ref[:, i * EIGHTH : (i + 1) * EIGHTH] = mixed[i].astype(BF16)

    landing(packed.at[pl.ds(1, 7)], sent.at[0])
    landing(xs.at[pl.ds(0, 480)], sent.at[1])
    landing(parts.at[pl.ds(0, 480)], sent.at[2])
    landing(back.at[pl.ds(0, 15)], sent.at[3])


def local(
    queries, cached_keys, cached_values, lengths, norm_gain,
    expert_ids, gates, gate_proj, up_proj, down_proj,
):
    vmem = pl.BlockSpec(memory_space=pltpu.VMEM)
    hbm = pl.BlockSpec(memory_space=pl.ANY)
    dma = pltpu.SemaphoreType.DMA
    return pl.pallas_call(
        kernel,
        out_shape=jax.ShapeDtypeStruct((REQUESTS, HALF), BF16),
        in_specs=[hbm, hbm, hbm, hbm, hbm, hbm, hbm, hbm, hbm, hbm],
        out_specs=vmem,
        scratch_shapes=[
            pltpu.VMEM((REQUESTS, MODEL_WIDTH), BF16),
            pltpu.VMEM((1, MODEL_WIDTH), F32),
            pltpu.VMEM((2, REQUESTS), jnp.int32),
            pltpu.VMEM((2, REQUESTS), F32),
            pltpu.VMEM((REQUESTS, POSITIONS, WIDE), BF16),
            pltpu.VMEM((REQUESTS, POSITIONS, WIDE), BF16),
            pltpu.VMEM((MODEL_WIDTH, WIDE), BF16),
            pltpu.VMEM((MODEL_WIDTH, WIDE), BF16),
            pltpu.VMEM((WIDE, MODEL_WIDTH), BF16),
            pltpu.VMEM((REQUESTS * QUERY_HEADS, HEAD_WIDTH), F32),
            pltpu.VMEM((REQUESTS * QUERY_HEADS, HEAD_WIDTH), F32),
            pltpu.VMEM((REQUESTS * QUERY_HEADS, HEAD_WIDTH), F32),
            pltpu.VMEM((8, ROWS, QUARTER), BF16),
            pltpu.VMEM((8, ROWS, QUARTER), BF16),
            pltpu.VMEM((512, MODEL_WIDTH), BF16),
            pltpu.VMEM((128, WIDE), BF16),
            pltpu.VMEM((512, MODEL_WIDTH), BF16),
            pltpu.VMEM((2, 4, ROWS, MODEL_WIDTH), BF16),
            pltpu.VMEM((2, 4, 2, ROWS, MODEL_WIDTH), BF16),
            pltpu.VMEM((2, 3, ROWS, MODEL_WIDTH), BF16),
            pltpu.VMEM((16, ROWS, EIGHTH), BF16),
            pltpu.VMEM((16, ROWS, EIGHTH), BF16),
            pltpu.VMEM((128, 256), BF16),
            pltpu.SMEM((REQUESTS,), jnp.int32),
            dma((16,)), dma((4,)), dma((2,)), dma((16,)), dma((18,)), dma((2,)),
        ],
        compiler_params=pltpu.CompilerParams(
            collective_id=0, has_side_effects=True, vmem_limit_bytes=56 * 1024 * 1024
        ),
        cost_estimate=pl.CostEstimate(
            flops=5_000_000_000, bytes_accessed=14_000_000, transcendentals=400_000
        ),
    )(
        queries, cached_keys, cached_values, lengths, norm_gain.reshape(1, MODEL_WIDTH),
        expert_ids.T, gates.T, gate_proj, up_proj, down_proj,
    )


def solution(mesh):
    placed = (
        P(("grp", "tp"), None),
        P(("grp", "tp"), None, None),
        P(("grp", "tp"), None, None),
        P(("grp", "tp")),
        P(),
        P(("grp", "tp"), None),
        P(("grp", "tp"), None),
        P("grp", None, "tp"),
        P("grp", None, "tp"),
        P("grp", "tp", None),
    )
    return jax.shard_map(
        local, mesh=mesh, in_specs=placed, out_specs=P(("grp", "tp"), "role"), check_vma=False
    )
```

```python
import functools
import math

import jax
import jax.numpy as jnp
from jax import lax
from jax.experimental import pallas as pl
from jax.experimental.pallas import tpu as pltpu
from jax.sharding import PartitionSpec as P

HEAD_WIDTH = 128
QUERY_HEADS = 24
KEY_VALUE_HEADS = 4
MODEL_WIDTH = 3072
REQUESTS = 16
POSITIONS = 128
WIDE = 512
QUARTER = 768
HALF = 1536
EIGHTH = 384
ROWS = 16
OFFSETS = (0, 1, -1, 2, -2, 3, -3, 4)
MIX = (1, 0)
FIRST_BLOCK = 0
ORDER = (
    ("unpack", 0), ("own", 0, 0, 1), ("own", 0, 0, -1), ("own", 0, 1, 1), ("own", 0, 1, -1),
    ("unpack", 1), ("own", 1, 0, 1), ("own", 1, 0, -1), ("own", 1, 1, 1), ("own", 1, 1, -1),
    ("far", 0), ("across", 0, 1, 1), ("across", 0, 1, -1), ("far", 1), ("across", 1, 1, 1),
    ("across", 1, 1, -1), ("across", 0, 3, 1), ("across", 0, 3, -1), ("across", 1, 3, 1),
    ("across", 1, 3, -1), ("pass", 0, 0), ("pass", 1, 0), ("across", 0, 2, 1),
    ("across", 0, 2, -1), ("across", 1, 2, 1), ("across", 1, 2, -1), ("experts", 0),
    ("down", 0, 0), ("down", 0, 1), ("pass", 0, 1), ("pass", 1, 1), ("pass", 0, 3),
    ("pass", 1, 3), ("pass", 0, 2), ("pass", 1, 2), ("experts", 3), ("down", 3, 0),
    ("down", 3, 1), ("direct", 1, 0, 2), ("direct", 0, 0, 2), ("direct", 1, 0, 1),
    ("direct", 0, 0, 1), ("direct", 1, 0, 3), ("direct", 0, 0, 3), ("direct", 1, 0, 0),
    ("direct", 0, 0, 0), ("direct", 1, 1, 2), ("direct", 0, 1, 2), ("direct", 1, 1, 1),
    ("direct", 0, 1, 1), ("direct", 1, 1, 3), ("direct", 0, 1, 3), ("direct", 1, 1, 0),
    ("direct", 0, 1, 0), ("experts", 1), ("down", 1, 0), ("down", 1, 1), ("experts", 2),
    ("down", 2, 0), ("opposite", 1, 0, 2), ("opposite", 0, 0, 2), ("opposite", 1, 0, 1),
    ("opposite", 0, 0, 1), ("opposite", 1, 0, 3), ("opposite", 0, 0, 3), ("opposite", 1, 0, 0),
    ("opposite", 0, 0, 0), ("down", 2, 1), ("opposite", 1, 1, 2), ("opposite", 0, 1, 2),
    ("opposite", 1, 1, 1), ("opposite", 0, 1, 1), ("opposite", 1, 1, 3), ("opposite", 0, 1, 3),
    ("opposite", 1, 1, 0), ("opposite", 0, 1, 0), ("sum", 1, 0, 2), ("sum", 0, 0, 2),
    ("sum", 1, 0, 1), ("sum", 0, 0, 1), ("sum", 1, 0, 3), ("sum", 0, 0, 3), ("sum", 1, 0, 0),
    ("sum", 0, 0, 0), ("sum", 1, 1, 2), ("sum", 0, 1, 2), ("sum", 1, 1, 1), ("sum", 0, 1, 1),
    ("sum", 1, 1, 3), ("sum", 0, 1, 3), ("sum", 1, 1, 0), ("sum", 0, 1, 0), ("line", 1, 0, 2),
    ("line", 0, 0, 2), ("line", 1, 0, 1), ("line", 0, 0, 1), ("line", 1, 0, 3), ("line", 0, 0, 3),
    ("line", 1, 0, 0), ("line", 0, 0, 0), ("line", 1, 1, 2), ("line", 0, 1, 2), ("line", 1, 1, 1),
    ("line", 0, 1, 1), ("line", 1, 1, 3), ("line", 0, 1, 3), ("line", 1, 1, 0), ("line", 0, 1, 0),
    ("give", 1, 0), ("give", 0, 0), ("give", 1, 1), ("give", 0, 1),
)
MESH = pl.DeviceIdType.MESH
F32 = jnp.float32
BF16 = jnp.bfloat16


def iota(shape, axis):
    return lax.broadcasted_iota(jnp.int32, shape, axis)


def one_hot(mask):
    return jnp.where(mask, 1.0, 0.0).astype(BF16)


def dot(a, b):
    return jnp.dot(a, b, preferred_element_type=F32)


def offset_of(index):
    step = (index + 1) // 2
    return jnp.where(index % 2 == 1, step, -step)


def kernel(
    q_hbm, k_hbm, v_hbm, len_hbm, gain_hbm, ids_hbm, gates_hbm, wg_hbm, wu_hbm, wd_hbm,
    out_ref,
    q_buf, gain, ids, gates, k_buf, v_buf, wg, wu, wd, q_rows, s_rows, c_rows,
    packed, landed, xs, hidden, parts, r1, r2, r3, back, home, table, lengths,
    local_sem, sent, z_recv, ag_recv, rs_recv, ret_recv,
):
    role = lax.axis_index("role")
    z = lax.axis_index("grp")
    t = lax.axis_index("tp")
    x, y = t % 4, t // 4
    turn = 1 - 2 * role

    def at(w, axis, step):
        along_x = int(axis == w)
        col = (x + step * turn * along_x + 4) % 4
        row = (y + step * turn * (1 - along_x) + 4) % 4
        return (role, z, row * 4 + col)

    def at_z(step, core):
        return (core, (z + step + 8) % 8, t)

    barrier = pltpu.get_barrier_semaphore()
    partners = [at(0, a, step) for a in (0, 1) for step in (1, -1, 2)] + [at_z(0, 1 - role)]
    for step in OFFSETS[1:]:
        partners += [at_z(step, role), at_z(step, 1 - role)]
    for partner in partners:
        pl.semaphore_signal(barrier, inc=1, device_id=partner, device_id_type=MESH)

    small = [
        pltpu.make_async_copy(src, dst, local_sem.at[i])
        for i, (src, dst) in enumerate(
            ((q_hbm, q_buf), (len_hbm, lengths), (ids_hbm, ids), (gain_hbm, gain),
             (gates_hbm, gates))
        )
    ]
    loads = []
    for i in range(4):
        rows = pl.ds(4 * i, 4)
        loads.append((
            pltpu.make_async_copy(k_hbm.at[rows], k_buf.at[rows], local_sem.at[8 + i]),
            pltpu.make_async_copy(v_hbm.at[rows], v_buf.at[rows], local_sem.at[12 + i]),
        ))
    weight_loads = [
        pltpu.make_async_copy(src.at[0], dst, local_sem.at[5 + i])
        for i, (src, dst) in enumerate(((wg_hbm, wg), (wu_hbm, wu), (wd_hbm, wd)))
    ]
    small[0].start()
    small[1].start()
    for kc, _ in loads:
        kc.start()
    for _, vc in loads:
        vc.start()
    for copy in small[2:]:
        copy.start()

    small[0].wait()
    for h in range(QUERY_HEADS):
        q_rows[pl.ds(h, REQUESTS, stride=QUERY_HEADS), :] = q_buf[
            :, h * HEAD_WIDTH : (h + 1) * HEAD_WIDTH
        ].astype(F32)
    small[1].wait()
    group = iota((QUERY_HEADS, HEAD_WIDTH), 0) // (QUERY_HEADS // KEY_VALUE_HEADS)
    place = iota((QUERY_HEADS, POSITIONS), 1)
    scale = 1.0 / math.sqrt(HEAD_WIDTH)
    for r in range(REQUESTS):
        if r % 4 == 0:
            loads[r // 4][0].wait()
        own = q_rows[r * QUERY_HEADS : (r + 1) * QUERY_HEADS, :]
        spread = jnp.concatenate(
            [jnp.where(group == j, own, 0.0) for j in range(KEY_VALUE_HEADS)], axis=1
        ).astype(BF16)
        scores = lax.dot_general(
            spread, k_buf[r], (((1,), (1,)), ((), ())), preferred_element_type=F32
        )
        s_rows[r * QUERY_HEADS : (r + 1) * QUERY_HEADS, :] = jnp.where(
            place < lengths[r], scores * scale, -jnp.inf
        )
    for wc in weight_loads:
        wc.start()
    scores = s_rows[...]
    raised = jnp.exp(scores - jnp.max(scores, axis=1, keepdims=True))
    s_rows[...] = raised / jnp.sum(raised, axis=1, keepdims=True)
    for r in range(REQUESTS):
        if r % 4 == 0:
            loads[r // 4][1].wait()
        weights = s_rows[r * QUERY_HEADS : (r + 1) * QUERY_HEADS, :].astype(BF16)
        mixed = dot(weights, v_buf[r])
        own = jnp.where(group == 0, mixed[:, :HEAD_WIDTH], 0.0)
        for j in range(1, KEY_VALUE_HEADS):
            own = jnp.where(group == j, mixed[:, j * HEAD_WIDTH : (j + 1) * HEAD_WIDTH], own)
        c_rows[r * QUERY_HEADS : (r + 1) * QUERY_HEADS, :] = own
    for copy in small[2:]:
        copy.wait()
    heads = [
        c_rows[pl.ds(h, REQUESTS, stride=QUERY_HEADS), :] for h in range(QUERY_HEADS)
    ]
    squares = heads[0] * heads[0]
    for head in heads[1:]:
        squares = squares + head * head
    mean_square = jnp.sum(squares, axis=1, keepdims=True) / MODEL_WIDTH
    norm = lax.rsqrt(mean_square + 1e-05)
    expert_in = [
        head * norm * gain[:, h * HEAD_WIDTH : (h + 1) * HEAD_WIDTH]
        for h, head in enumerate(heads)
    ]
    stacked = jnp.concatenate(
        [jnp.concatenate(expert_in[6 * i : 6 * i + 6], axis=1) for i in range(4)], axis=0
    ).astype(BF16)

    diagonal = iota((16, 16), 0) == iota((16, 16), 1)
    first = jnp.concatenate([ids[0:1, :]] * 4, axis=1)
    second = jnp.concatenate([ids[1:2, :]] * 4, axis=1)
    row, col = iota((128, 64), 0), iota((128, 64), 1)
    expert = (z + turn * offset_of(row // 16) + 8) % 8
    hit = (first == expert) | (second == expert)
    trow, tcol = iota((64, 64), 0), iota((64, 64), 1)
    earlier = (trow // 16 == tcol // 16) & (trow % 16 < tcol % 16)
    rank = dot(one_hot(hit), one_hot(earlier))
    slot = ((row // 4) % 4 + 4 * role).astype(F32)
    chosen = one_hot(hit & (rank == slot) & (row % 4 == col // 16))
    packets = dot(chosen, stacked).astype(BF16)
    packed[...] = packets.reshape(8, ROWS, QUARTER)

    pl.semaphore_wait(barrier, len(partners))

    def landing(ref, sem):
        pltpu.make_async_copy(ref, ref, sem).wait()

    for j in (1, 2, 3, 7, 5, 6, 4):
        pltpu.make_async_remote_copy(
            src_ref=packed.at[j], dst_ref=landed.at[j],
            send_sem=sent.at[0], recv_sem=z_recv.at[j // 4],
            device_id=at_z(turn * OFFSETS[j], role), device_id_type=MESH,
        ).start()
    landed[0] = packets[:ROWS]

    def block(ref, w, u, v):
        return ref.at[pl.ds((v * 8 + w * 4 + u) * ROWS, ROWS), :]

    def gather(w, axis, step, u, v):
        du, dv = ((u + step) % 4, v) if axis == 0 else (u, (v + step) % 4)
        number = (w * 3 + du - 1, 6 + w * 4 + du, 14, 15)[dv]
        pltpu.make_async_remote_copy(
            src_ref=block(xs, w, u, v), dst_ref=block(xs, w, du, dv),
            send_sem=sent.at[1], recv_sem=ag_recv.at[number],
            device_id=at(w, axis, step), device_id_type=MESH,
        ).start()

    seen = set()

    def arrived(w, u, v):
        if (w, u, v) not in seen:
            seen.add((w, u, v))
            landing(block(xs, w, u, v), ag_recv.at[w * 3 + u - 1 if v == 0 else 6 + w * 4 + u])

    pick_row, pick_col = iota((64, 64), 0), iota((64, 64), 1)
    picks = one_hot((pick_col // 4 == pick_row % 16) & (pick_col % 4 == pick_row // 16))

    def unpack(w):
        first = max(4 * w, 1)
        landing(landed.at[pl.ds(first, 4 * w + 4 - first)], z_recv.at[w])
        rows = dot(picks, landed[4 * w : 4 * w + 4].reshape(64, QUARTER)).astype(BF16)
        low = 4 * w * ROWS
        for i in range(4):
            xs[low : low + ROWS, i * QUARTER : (i + 1) * QUARTER] = rows[
                i * ROWS : (i + 1) * ROWS
            ]

    def own(w, axis, step):
        gather(w, axis, step, 0, 0)

    def far(w):
        arrived(w, 1, 0)
        gather(w, 0, 1, 1, 0)

    def across(w, u, step):
        arrived(w, u, 0)
        gather(w, 1, step, u, 0)

    def pass_on(w, u):
        arrived(w, u, 1)
        gather(w, 1, 1, u, 1)

    def experts(v):
        if v == FIRST_BLOCK:
            for wc in weight_loads:
                wc.wait()
        low = v * 128
        if v > 1:
            landing(xs.at[pl.ds(low, 128)], ag_recv.at[12 + v])
        else:
            for w in range(2):
                for u in range(1 - v, 4):
                    arrived(w, u, v)
        for n in range(2):
            cols = slice(n * 256, (n + 1) * 256)
            gate = dot(xs[low : low + 128], wg[:, cols])
            up = dot(xs[low : low + 128], wu[:, cols])
            hidden[:, cols] = (gate / (1.0 + jnp.exp(-gate)) * up).astype(BF16)

    def down(v, h):
        low = v * 128
        for n in range(3 * h, 3 * h + 3):
            cols = slice(n * 512, (n + 1) * 512)
            parts[low : low + 128, cols] = dot(hidden[...], wd[:, cols]).astype(BF16)


    def half_block(w, h, u, v):
        return block(parts, w, u, v).at[:, pl.ds(h * HALF, HALF)]

    def send_sum(src, dst, number, w, axis, step):
        pltpu.make_async_remote_copy(
            src_ref=src, dst_ref=dst, send_sem=sent.at[2], recv_sem=rs_recv.at[number],
            device_id=at(w, axis, step), device_id_type=MESH,
        ).start()

    def sum_direct(w, h, u):
        number = 16 + (w * 2 + h) * 4 + u
        send_sum(half_block(w, h, u, 3), r2.at[w, h, u, 0], number, w, 1, 1)

    def sum_opposite(w, h, u):
        number = (w * 2 + h) * 4 + u
        send_sum(half_block(w, h, u, 2), r1.at[w, h, u], number, w, 1, -1)

    def sum_pass(w, h, u):
        number = (w * 2 + h) * 4 + u
        landing(r1.at[w, h, u], rs_recv.at[number])
        mine = half_block(w, h, u, 1)
        mine[...] = (mine[...].astype(F32) + r1[w, h, u].astype(F32)).astype(BF16)
        send_sum(mine, r2.at[w, h, u, 1], 16 + number, w, 1, -1)

    def sum_line(w, h, u):
        landing(r2.at[w, h, u], rs_recv.at[16 + (w * 2 + h) * 4 + u])
        mine = half_block(w, h, u, 0)
        mine[...] = (
            mine[...].astype(F32) + r2[w, h, u, 0].astype(F32) + r2[w, h, u, 1].astype(F32)
        ).astype(BF16)
        if u > 0:
            send_sum(mine, r3.at[w, h, u - 1], 32 + w * 2 + h, w, 0, (-1, 2, 1)[u - 1])

    spreads = one_hot((pick_row // 4 == pick_col % 16) & (pick_row % 4 == pick_col // 16))

    def give_back(w, h):
        landing(r3.at[w, h], rs_recv.at[32 + w * 2 + h])
        total = half_block(w, h, 0, 0)[...].astype(F32)
        for i in range(3):
            total = total + r3[w, h, i].astype(F32)
        total = total.astype(BF16)
        rows = jnp.concatenate(
            [total[:, i * EIGHTH : (i + 1) * EIGHTH] for i in range(4)], axis=0
        )
        low = h * 8 + 4 * w
        back[low : low + 4] = dot(spreads, rows).astype(BF16).reshape(4, ROWS, EIGHTH)
        for j in range(4 * w + 3, max(4 * w, 1) - 1, -1):
            other = role if h == 0 else 1 - role
            pltpu.make_async_remote_copy(
                src_ref=back.at[h * 8 + j], dst_ref=home.at[j * 2 + other],
                send_sem=sent.at[3], recv_sem=ret_recv.at[w],
                device_id=at_z(-turn * OFFSETS[j], h), device_id_type=MESH,
            ).start()
        if w == 0:
            given.append(h)
        if w == 0 and len(given) == 2:
            home[0] = back[role * 8]
            pltpu.make_async_remote_copy(
                src_ref=back.at[(1 - role) * 8], dst_ref=home.at[1],
                send_sem=sent.at[3], recv_sem=ret_recv.at[0],
                device_id=at_z(0, 1 - role), device_id_type=MESH,
            ).start()

    given = []

    def mix_table():
        row, col = iota((128, 256), 0), iota((128, 256), 1)
        other = (col // 16) % 2
        core = role + other - 2 * role * other
        expert = (z + (1 - 2 * core) * offset_of(col // 32) + 8) % 8
        names = [
            jnp.sum(jnp.where(diagonal, ids[k : k + 1, :], 0), axis=1, keepdims=True)
            for k in range(2)
        ]
        names = [jnp.concatenate([name] * 8, axis=0) for name in names]
        hit = (names[0] == expert) | (names[1] == expert)
        trow, tcol = iota((128, 128), 0), iota((128, 128), 1)
        before = one_hot((trow // 16 == tcol // 16) & (tcol < trow))
        rank = dot(before, one_hot(hit))
        fits = (rank == (col % 16 // 4 + 4 * core).astype(F32)) & (col % 4 == (row // 16) % 4)
        named = jnp.where(row < 64, names[0], names[1]) == expert
        table[...] = one_hot(named & fits)

    def mix(w, so_far):
        first = max(8 * w, 1)
        landing(home.at[pl.ds(first, 8 * w + 8 - first)], ret_recv.at[w])
        rows = home[8 * w : 8 * w + 8].reshape(128, EIGHTH)
        terms = dot(table[:, 128 * w : 128 * w + 128], rows)
        new = []
        for i in range(4):
            total = so_far[i] if so_far else 0.0
            for k in range(2):
                low = (k * 4 + i) * ROWS
                total = total + terms[low : low + ROWS] * weight[k]
            new.append(total)
        return new

    weight = [
        jnp.sum(jnp.where(diagonal, gates[k : k + 1, :], 0.0), axis=1, keepdims=True)
        for k in range(2)
    ]

    steps = {
        "unpack": unpack, "own": own, "far": far, "across": across, "pass": pass_on,
        "experts": experts, "down": down, "direct": sum_direct, "opposite": sum_opposite, "sum": sum_pass,
        "line": sum_line, "give": give_back,
    }
    mix_table()
    for name, *where in ORDER:
        steps[name](*where)
    mixed = mix(MIX[1], mix(MIX[0], None))
    for i in range(4):
        out_ref[:, i * EIGHTH : (i + 1) * EIGHTH] = mixed[i].astype(BF16)

    landing(packed.at[pl.ds(1, 7)], sent.at[0])
    landing(xs.at[pl.ds(0, 480)], sent.at[1])
    landing(parts.at[pl.ds(0, 480)], sent.at[2])
    landing(back.at[pl.ds(0, 15)], sent.at[3])


def local(
    queries, cached_keys, cached_values, lengths, norm_gain,
    expert_ids, gates, gate_proj, up_proj, down_proj,
):
    vmem = pl.BlockSpec(memory_space=pltpu.VMEM)
    hbm = pl.BlockSpec(memory_space=pl.ANY)
    dma = pltpu.SemaphoreType.DMA
    return pl.pallas_call(
        kernel,
        out_shape=jax.ShapeDtypeStruct((REQUESTS, HALF), BF16),
        in_specs=[hbm, hbm, hbm, hbm, hbm, hbm, hbm, hbm, hbm, hbm],
        out_specs=vmem,
        scratch_shapes=[
            pltpu.VMEM((REQUESTS, MODEL_WIDTH), BF16),
            pltpu.VMEM((1, MODEL_WIDTH), F32),
            pltpu.VMEM((2, REQUESTS), jnp.int32),
            pltpu.VMEM((2, REQUESTS), F32),
            pltpu.VMEM((REQUESTS, POSITIONS, WIDE), BF16),
            pltpu.VMEM((REQUESTS, POSITIONS, WIDE), BF16),
            pltpu.VMEM((MODEL_WIDTH, WIDE), BF16),
            pltpu.VMEM((MODEL_WIDTH, WIDE), BF16),
            pltpu.VMEM((WIDE, MODEL_WIDTH), BF16),
            pltpu.VMEM((REQUESTS * QUERY_HEADS, HEAD_WIDTH), F32),
            pltpu.VMEM((REQUESTS * QUERY_HEADS, HEAD_WIDTH), F32),
            pltpu.VMEM((REQUESTS * QUERY_HEADS, HEAD_WIDTH), F32),
            pltpu.VMEM((8, ROWS, QUARTER), BF16),
            pltpu.VMEM((8, ROWS, QUARTER), BF16),
            pltpu.VMEM((512, MODEL_WIDTH), BF16),
            pltpu.VMEM((128, WIDE), BF16),
            pltpu.VMEM((512, MODEL_WIDTH), BF16),
            pltpu.VMEM((2, 2, 4, ROWS, HALF), BF16),
            pltpu.VMEM((2, 2, 4, 2, ROWS, HALF), BF16),
            pltpu.VMEM((2, 2, 3, ROWS, HALF), BF16),
            pltpu.VMEM((16, ROWS, EIGHTH), BF16),
            pltpu.VMEM((16, ROWS, EIGHTH), BF16),
            pltpu.VMEM((128, 256), BF16),
            pltpu.SMEM((REQUESTS,), jnp.int32),
            dma((16,)), dma((4,)), dma((2,)), dma((16,)), dma((36,)), dma((2,)),
        ],
        compiler_params=pltpu.CompilerParams(
            collective_id=0, has_side_effects=True, vmem_limit_bytes=56 * 1024 * 1024
        ),
        cost_estimate=pl.CostEstimate(
            flops=5_000_000_000, bytes_accessed=14_000_000, transcendentals=400_000
        ),
    )(
        queries, cached_keys, cached_values, lengths, norm_gain.reshape(1, MODEL_WIDTH),
        expert_ids.T, gates.T, gate_proj, up_proj, down_proj,
    )


def solution(mesh):
    placed = (
        P(("grp", "tp"), None),
        P(("grp", "tp"), None, None),
        P(("grp", "tp"), None, None),
        P(("grp", "tp")),
        P(),
        P(("grp", "tp"), None),
        P(("grp", "tp"), None),
        P("grp", None, "tp"),
        P("grp", None, "tp"),
        P("grp", "tp", None),
    )
    return jax.shard_map(
        local, mesh=mesh, in_specs=placed, out_specs=P(("grp", "tp"), "role"), check_vma=False
    )
```

```python
import functools
import math

import jax
import jax.numpy as jnp
from jax import lax
from jax.experimental import pallas as pl
from jax.experimental.pallas import tpu as pltpu
from jax.sharding import PartitionSpec as P

HEAD_WIDTH = 128
QUERY_HEADS = 24
KEY_VALUE_HEADS = 4
MODEL_WIDTH = 3072
REQUESTS = 16
POSITIONS = 128
WIDE = 512
QUARTER = 768
HALF = 1536
EIGHTH = 384
ROWS = 16
OFFSETS = (0, 1, -1, 2, -2, 3, -3, 4)
MIX = (1, 0)
FIRST_BLOCK = 0
ORDER = (
    ("unpack", 0), ("own", 0, 0, 1), ("own", 0, 0, -1), ("own", 0, 1, 1), ("own", 0, 1, -1),
    ("unpack", 1), ("own", 1, 0, 1), ("own", 1, 0, -1), ("own", 1, 1, 1), ("own", 1, 1, -1),
    ("far", 0), ("across", 0, 1, 1), ("across", 0, 1, -1), ("far", 1), ("across", 1, 1, 1),
    ("across", 1, 1, -1), ("across", 0, 3, 1), ("across", 0, 3, -1), ("across", 1, 3, 1),
    ("across", 1, 3, -1), ("pass", 0, 0), ("pass", 1, 0), ("across", 0, 2, 1),
    ("across", 0, 2, -1), ("across", 1, 2, 1), ("across", 1, 2, -1), ("experts", 0),
    ("pass", 0, 1), ("pass", 1, 1), ("down", 0, 0), ("down", 0, 1), ("pass", 0, 3),
    ("pass", 1, 3), ("pass", 0, 2), ("pass", 1, 2), ("experts", 3), ("down", 3, 0),
    ("down", 3, 1), ("direct", 1, 0, 2), ("direct", 0, 0, 2), ("direct", 1, 0, 1),
    ("direct", 0, 0, 1), ("direct", 1, 0, 3), ("direct", 0, 0, 3), ("direct", 1, 0, 0),
    ("direct", 0, 0, 0), ("direct", 1, 1, 2), ("direct", 0, 1, 2), ("direct", 1, 1, 1),
    ("direct", 0, 1, 1), ("direct", 1, 1, 3), ("direct", 0, 1, 3), ("direct", 1, 1, 0),
    ("direct", 0, 1, 0), ("experts", 2), ("down", 2, 0), ("opposite", 1, 0, 2),
    ("opposite", 0, 0, 2), ("opposite", 1, 0, 1), ("opposite", 0, 0, 1), ("opposite", 1, 0, 3),
    ("opposite", 0, 0, 3), ("opposite", 1, 0, 0), ("opposite", 0, 0, 0), ("down", 2, 1),
    ("opposite", 1, 1, 2), ("opposite", 0, 1, 2), ("opposite", 1, 1, 1), ("opposite", 0, 1, 1),
    ("opposite", 1, 1, 3), ("opposite", 0, 1, 3), ("opposite", 1, 1, 0), ("opposite", 0, 1, 0),
    ("experts", 1), ("down", 1, 0), ("down", 1, 1), ("sum", 1, 0, 2), ("sum", 0, 0, 2),
    ("sum", 1, 0, 1), ("sum", 0, 0, 1), ("sum", 1, 0, 3), ("sum", 0, 0, 3), ("sum", 1, 0, 0),
    ("sum", 0, 0, 0), ("sum", 1, 1, 2), ("sum", 0, 1, 2), ("sum", 1, 1, 1), ("sum", 0, 1, 1),
    ("sum", 1, 1, 3), ("sum", 0, 1, 3), ("sum", 1, 1, 0), ("sum", 0, 1, 0), ("line", 1, 0, 2),
    ("line", 0, 0, 2), ("line", 1, 0, 1), ("line", 0, 0, 1), ("line", 1, 0, 3), ("line", 0, 0, 3),
    ("line", 1, 0, 0), ("line", 0, 0, 0), ("line", 1, 1, 2), ("line", 0, 1, 2), ("line", 1, 1, 1),
    ("line", 0, 1, 1), ("line", 1, 1, 3), ("line", 0, 1, 3), ("line", 1, 1, 0), ("line", 0, 1, 0),
    ("give", 1, 0), ("give", 0, 0), ("give", 1, 1), ("give", 0, 1),
)
MESH = pl.DeviceIdType.MESH
F32 = jnp.float32
BF16 = jnp.bfloat16


def iota(shape, axis):
    return lax.broadcasted_iota(jnp.int32, shape, axis)


def one_hot(mask):
    return jnp.where(mask, 1.0, 0.0).astype(BF16)


def dot(a, b):
    return jnp.dot(a, b, preferred_element_type=F32)


def offset_of(index):
    step = (index + 1) // 2
    return jnp.where(index % 2 == 1, step, -step)


def kernel(
    q_hbm, k_hbm, v_hbm, len_hbm, gain_hbm, ids_hbm, gates_hbm, wg_hbm, wu_hbm, wd_hbm,
    out_ref,
    q_buf, gain, ids, gates, k_buf, v_buf, wg, wu, wd, q_rows, s_rows, c_rows,
    packed, landed, xs, hidden, parts, r1, r2, r3, back, home, table, chosen, lengths,
    local_sem, sent, z_recv, ag_recv, rs_recv, ret_recv,
):
    role = lax.axis_index("role")
    z = lax.axis_index("grp")
    t = lax.axis_index("tp")
    x, y = t % 4, t // 4
    turn = 1 - 2 * role

    def at(w, axis, step):
        along_x = int(axis == w)
        col = (x + step * turn * along_x + 4) % 4
        row = (y + step * turn * (1 - along_x) + 4) % 4
        return (role, z, row * 4 + col)

    def at_z(step, core):
        return (core, (z + step + 8) % 8, t)

    barrier = pltpu.get_barrier_semaphore()
    partners = []
    for step in OFFSETS[:0:-1]:
        partners += [at_z(step, role), at_z(step, 1 - role)]
    partners += [at(0, a, step) for a in (0, 1) for step in (2, 1, -1)] + [at_z(0, 1 - role)]
    for partner in partners:
        pl.semaphore_signal(barrier, inc=1, device_id=partner, device_id_type=MESH)

    small = [
        pltpu.make_async_copy(src, dst, local_sem.at[i])
        for i, (src, dst) in enumerate(
            ((q_hbm, q_buf), (len_hbm, lengths), (ids_hbm, ids), (gain_hbm, gain),
             (gates_hbm, gates))
        )
    ]
    loads = []
    for i in range(4):
        rows = pl.ds(4 * i, 4)
        loads.append((
            pltpu.make_async_copy(k_hbm.at[rows], k_buf.at[rows], local_sem.at[8 + i]),
            pltpu.make_async_copy(v_hbm.at[rows], v_buf.at[rows], local_sem.at[12 + i]),
        ))
    weight_loads = [
        pltpu.make_async_copy(src.at[0], dst, local_sem.at[5 + i])
        for i, (src, dst) in enumerate(((wg_hbm, wg), (wu_hbm, wu), (wd_hbm, wd)))
    ]
    small[0].start()
    small[1].start()
    small[2].start()
    for kc, _ in loads:
        kc.start()
    for _, vc in loads:
        vc.start()
    for copy in small[3:]:
        copy.start()

    small[0].wait()
    for h in range(QUERY_HEADS):
        q_rows[pl.ds(h, REQUESTS, stride=QUERY_HEADS), :] = q_buf[
            :, h * HEAD_WIDTH : (h + 1) * HEAD_WIDTH
        ].astype(F32)
    small[1].wait()
    group = iota((QUERY_HEADS, HEAD_WIDTH), 0) // (QUERY_HEADS // KEY_VALUE_HEADS)
    place = iota((QUERY_HEADS, POSITIONS), 1)
    scale = 1.0 / math.sqrt(HEAD_WIDTH)
    for r in range(REQUESTS):
        if r % 4 == 0:
            loads[r // 4][0].wait()
        own = q_rows[r * QUERY_HEADS : (r + 1) * QUERY_HEADS, :]
        spread = jnp.concatenate(
            [jnp.where(group == j, own, 0.0) for j in range(KEY_VALUE_HEADS)], axis=1
        ).astype(BF16)
        scores = lax.dot_general(
            spread, k_buf[r], (((1,), (1,)), ((), ())), preferred_element_type=F32
        )
        s_rows[r * QUERY_HEADS : (r + 1) * QUERY_HEADS, :] = jnp.where(
            place < lengths[r], scores * scale, -jnp.inf
        )
    for wc in weight_loads:
        wc.start()
    for copy in small[2:]:
        copy.wait()
    diagonal = iota((16, 16), 0) == iota((16, 16), 1)
    first = jnp.concatenate([ids[0:1, :]] * 4, axis=1)
    second = jnp.concatenate([ids[1:2, :]] * 4, axis=1)
    row, col = iota((128, 64), 0), iota((128, 64), 1)
    expert = (z + turn * offset_of(row // 16) + 8) % 8
    hit = (first == expert) | (second == expert)
    trow, tcol = iota((64, 64), 0), iota((64, 64), 1)
    earlier = (trow // 16 == tcol // 16) & (trow % 16 < tcol % 16)
    rank = dot(one_hot(hit), one_hot(earlier))
    slot = ((row // 4) % 4 + 4 * role).astype(F32)
    chosen[...] = one_hot(hit & (rank == slot) & (row % 4 == col // 16))

    scores = s_rows[...]
    raised = jnp.exp(scores - jnp.max(scores, axis=1, keepdims=True))
    s_rows[...] = raised / jnp.sum(raised, axis=1, keepdims=True)
    for r in range(REQUESTS):
        if r % 4 == 0:
            loads[r // 4][1].wait()
        weights = s_rows[r * QUERY_HEADS : (r + 1) * QUERY_HEADS, :].astype(BF16)
        mixed = dot(weights, v_buf[r])
        own = jnp.where(group == 0, mixed[:, :HEAD_WIDTH], 0.0)
        for j in range(1, KEY_VALUE_HEADS):
            own = jnp.where(group == j, mixed[:, j * HEAD_WIDTH : (j + 1) * HEAD_WIDTH], own)
        c_rows[r * QUERY_HEADS : (r + 1) * QUERY_HEADS, :] = own
    heads = [
        c_rows[pl.ds(h, REQUESTS, stride=QUERY_HEADS), :] for h in range(QUERY_HEADS)
    ]
    squares = heads[0] * heads[0]
    for head in heads[1:]:
        squares = squares + head * head
    mean_square = jnp.sum(squares, axis=1, keepdims=True) / MODEL_WIDTH
    norm = lax.rsqrt(mean_square + 1e-05)
    expert_in = [
        head * norm * gain[:, h * HEAD_WIDTH : (h + 1) * HEAD_WIDTH]
        for h, head in enumerate(heads)
    ]
    stacked = jnp.concatenate(
        [jnp.concatenate(expert_in[6 * i : 6 * i + 6], axis=1) for i in range(4)], axis=0
    ).astype(BF16)

    def landing(ref, sem):
        pltpu.make_async_copy(ref, ref, sem).wait()

    def dispatch(w):
        packets = dot(chosen[64 * w : 64 * w + 64], stacked).astype(BF16)
        packed[4 * w : 4 * w + 4] = packets.reshape(4, ROWS, QUARTER)
        if w == 0:
            landed[0] = packets[:ROWS]
            pl.semaphore_wait(barrier, len(partners))
        for j in ((1, 2, 3), (7, 5, 6, 4))[w]:
            pltpu.make_async_remote_copy(
                src_ref=packed.at[j], dst_ref=landed.at[j],
                send_sem=sent.at[0], recv_sem=z_recv.at[w],
                device_id=at_z(turn * OFFSETS[j], role), device_id_type=MESH,
            ).start()

    dispatch(0)
    dispatch(1)

    def block(ref, w, u, v):
        return ref.at[pl.ds((v * 8 + w * 4 + u) * ROWS, ROWS), :]

    def gather(w, axis, step, u, v):
        du, dv = ((u + step) % 4, v) if axis == 0 else (u, (v + step) % 4)
        number = (w * 3 + du - 1, 6 + w * 4 + du, 14, 15)[dv]
        pltpu.make_async_remote_copy(
            src_ref=block(xs, w, u, v), dst_ref=block(xs, w, du, dv),
            send_sem=sent.at[1], recv_sem=ag_recv.at[number],
            device_id=at(w, axis, step), device_id_type=MESH,
        ).start()

    seen = set()

    def arrived(w, u, v):
        if (w, u, v) not in seen:
            seen.add((w, u, v))
            landing(block(xs, w, u, v), ag_recv.at[w * 3 + u - 1 if v == 0 else 6 + w * 4 + u])

    pick_row, pick_col = iota((64, 64), 0), iota((64, 64), 1)
    picks = one_hot((pick_col // 4 == pick_row % 16) & (pick_col % 4 == pick_row // 16))

    def unpack(w):
        first = max(4 * w, 1)
        landing(landed.at[pl.ds(first, 4 * w + 4 - first)], z_recv.at[w])
        rows = dot(picks, landed[4 * w : 4 * w + 4].reshape(64, QUARTER)).astype(BF16)
        low = 4 * w * ROWS
        for i in range(4):
            xs[low : low + ROWS, i * QUARTER : (i + 1) * QUARTER] = rows[
                i * ROWS : (i + 1) * ROWS
            ]

    def own(w, axis, step):
        gather(w, axis, step, 0, 0)

    def far(w):
        arrived(w, 1, 0)
        gather(w, 0, 1, 1, 0)

    def across(w, u, step):
        arrived(w, u, 0)
        gather(w, 1, step, u, 0)

    def pass_on(w, u):
        arrived(w, u, 1)
        gather(w, 1, 1, u, 1)

    def experts(v):
        if v == FIRST_BLOCK:
            for wc in weight_loads:
                wc.wait()
        low = v * 128
        if v > 1:
            landing(xs.at[pl.ds(low, 128)], ag_recv.at[12 + v])
        else:
            for w in range(2):
                for u in range(1 - v, 4):
                    arrived(w, u, v)
        for n in range(2):
            cols = slice(n * 256, (n + 1) * 256)
            gate = dot(xs[low : low + 128], wg[:, cols])
            up = dot(xs[low : low + 128], wu[:, cols])
            hidden[:, cols] = (gate / (1.0 + jnp.exp(-gate)) * up).astype(BF16)

    def down(v, h):
        low = v * 128
        for n in range(3 * h, 3 * h + 3):
            cols = slice(n * 512, (n + 1) * 512)
            parts[low : low + 128, cols] = dot(hidden[...], wd[:, cols]).astype(BF16)


    def half_block(w, h, u, v):
        return block(parts, w, u, v).at[:, pl.ds(h * HALF, HALF)]

    def send_sum(src, dst, number, w, axis, step):
        pltpu.make_async_remote_copy(
            src_ref=src, dst_ref=dst, send_sem=sent.at[2], recv_sem=rs_recv.at[number],
            device_id=at(w, axis, step), device_id_type=MESH,
        ).start()

    def sum_direct(w, h, u):
        number = 16 + (w * 2 + h) * 4 + u
        send_sum(half_block(w, h, u, 3), r2.at[w, h, u, 0], number, w, 1, 1)

    def sum_opposite(w, h, u):
        number = (w * 2 + h) * 4 + u
        send_sum(half_block(w, h, u, 2), r1.at[w, h, u], number, w, 1, -1)

    def sum_pass(w, h, u):
        number = (w * 2 + h) * 4 + u
        landing(r1.at[w, h, u], rs_recv.at[number])
        mine = half_block(w, h, u, 1)
        mine[...] = (mine[...].astype(F32) + r1[w, h, u].astype(F32)).astype(BF16)
        send_sum(mine, r2.at[w, h, u, 1], 16 + number, w, 1, -1)

    def sum_line(w, h, u):
        landing(r2.at[w, h, u], rs_recv.at[16 + (w * 2 + h) * 4 + u])
        mine = half_block(w, h, u, 0)
        mine[...] = (
            mine[...].astype(F32) + r2[w, h, u, 0].astype(F32) + r2[w, h, u, 1].astype(F32)
        ).astype(BF16)
        if u > 0:
            send_sum(mine, r3.at[w, h, u - 1], 32 + w * 2 + h, w, 0, (-1, 2, 1)[u - 1])

    spreads = one_hot((pick_row // 4 == pick_col % 16) & (pick_row % 4 == pick_col // 16))

    def give_back(w, h):
        landing(r3.at[w, h], rs_recv.at[32 + w * 2 + h])
        total = half_block(w, h, 0, 0)[...].astype(F32)
        for i in range(3):
            total = total + r3[w, h, i].astype(F32)
        total = total.astype(BF16)
        rows = jnp.concatenate(
            [total[:, i * EIGHTH : (i + 1) * EIGHTH] for i in range(4)], axis=0
        )
        low = h * 8 + 4 * w
        back[low : low + 4] = dot(spreads, rows).astype(BF16).reshape(4, ROWS, EIGHTH)
        for j in range(4 * w + 3, max(4 * w, 1) - 1, -1):
            other = role if h == 0 else 1 - role
            pltpu.make_async_remote_copy(
                src_ref=back.at[h * 8 + j], dst_ref=home.at[j * 2 + other],
                send_sem=sent.at[3], recv_sem=ret_recv.at[w],
                device_id=at_z(-turn * OFFSETS[j], h), device_id_type=MESH,
            ).start()
        if w == 0:
            given.append(h)
        if w == 0 and len(given) == 2:
            home[0] = back[role * 8]
            pltpu.make_async_remote_copy(
                src_ref=back.at[(1 - role) * 8], dst_ref=home.at[1],
                send_sem=sent.at[3], recv_sem=ret_recv.at[0],
                device_id=at_z(0, 1 - role), device_id_type=MESH,
            ).start()

    given = []

    def mix_table():
        row, col = iota((128, 256), 0), iota((128, 256), 1)
        other = (col // 16) % 2
        core = role + other - 2 * role * other
        expert = (z + (1 - 2 * core) * offset_of(col // 32) + 8) % 8
        names = [
            jnp.sum(jnp.where(diagonal, ids[k : k + 1, :], 0), axis=1, keepdims=True)
            for k in range(2)
        ]
        names = [jnp.concatenate([name] * 8, axis=0) for name in names]
        hit = (names[0] == expert) | (names[1] == expert)
        trow, tcol = iota((128, 128), 0), iota((128, 128), 1)
        before = one_hot((trow // 16 == tcol // 16) & (tcol < trow))
        rank = dot(before, one_hot(hit))
        fits = (rank == (col % 16 // 4 + 4 * core).astype(F32)) & (col % 4 == (row // 16) % 4)
        named = jnp.where(row < 64, names[0], names[1]) == expert
        table[...] = one_hot(named & fits)

    def mix(w, so_far):
        first = max(8 * w, 1)
        landing(home.at[pl.ds(first, 8 * w + 8 - first)], ret_recv.at[w])
        rows = home[8 * w : 8 * w + 8].reshape(128, EIGHTH)
        terms = dot(table[:, 128 * w : 128 * w + 128], rows)
        new = []
        for i in range(4):
            total = so_far[i] if so_far else 0.0
            for k in range(2):
                low = (k * 4 + i) * ROWS
                total = total + terms[low : low + ROWS] * weight[k]
            new.append(total)
        return new

    weight = [
        jnp.sum(jnp.where(diagonal, gates[k : k + 1, :], 0.0), axis=1, keepdims=True)
        for k in range(2)
    ]

    steps = {
        "unpack": unpack, "own": own, "far": far, "across": across, "pass": pass_on,
        "experts": experts, "down": down, "direct": sum_direct, "opposite": sum_opposite, "sum": sum_pass,
        "line": sum_line, "give": give_back,
    }
    mix_table()
    for name, *where in ORDER:
        steps[name](*where)
    mixed = mix(MIX[1], mix(MIX[0], None))
    for i in range(4):
        out_ref[:, i * EIGHTH : (i + 1) * EIGHTH] = mixed[i].astype(BF16)

    landing(packed.at[pl.ds(1, 7)], sent.at[0])
    landing(xs.at[pl.ds(0, 480)], sent.at[1])
    landing(parts.at[pl.ds(0, 480)], sent.at[2])
    landing(back.at[pl.ds(0, 15)], sent.at[3])


def local(
    queries, cached_keys, cached_values, lengths, norm_gain,
    expert_ids, gates, gate_proj, up_proj, down_proj,
):
    vmem = pl.BlockSpec(memory_space=pltpu.VMEM)
    hbm = pl.BlockSpec(memory_space=pl.ANY)
    dma = pltpu.SemaphoreType.DMA
    return pl.pallas_call(
        kernel,
        out_shape=jax.ShapeDtypeStruct((REQUESTS, HALF), BF16),
        in_specs=[hbm, hbm, hbm, hbm, hbm, hbm, hbm, hbm, hbm, hbm],
        out_specs=vmem,
        scratch_shapes=[
            pltpu.VMEM((REQUESTS, MODEL_WIDTH), BF16),
            pltpu.VMEM((1, MODEL_WIDTH), F32),
            pltpu.VMEM((2, REQUESTS), jnp.int32),
            pltpu.VMEM((2, REQUESTS), F32),
            pltpu.VMEM((REQUESTS, POSITIONS, WIDE), BF16),
            pltpu.VMEM((REQUESTS, POSITIONS, WIDE), BF16),
            pltpu.VMEM((MODEL_WIDTH, WIDE), BF16),
            pltpu.VMEM((MODEL_WIDTH, WIDE), BF16),
            pltpu.VMEM((WIDE, MODEL_WIDTH), BF16),
            pltpu.VMEM((REQUESTS * QUERY_HEADS, HEAD_WIDTH), F32),
            pltpu.VMEM((REQUESTS * QUERY_HEADS, HEAD_WIDTH), F32),
            pltpu.VMEM((REQUESTS * QUERY_HEADS, HEAD_WIDTH), F32),
            pltpu.VMEM((8, ROWS, QUARTER), BF16),
            pltpu.VMEM((8, ROWS, QUARTER), BF16),
            pltpu.VMEM((512, MODEL_WIDTH), BF16),
            pltpu.VMEM((128, WIDE), BF16),
            pltpu.VMEM((512, MODEL_WIDTH), BF16),
            pltpu.VMEM((2, 2, 4, ROWS, HALF), BF16),
            pltpu.VMEM((2, 2, 4, 2, ROWS, HALF), BF16),
            pltpu.VMEM((2, 2, 3, ROWS, HALF), BF16),
            pltpu.VMEM((16, ROWS, EIGHTH), BF16),
            pltpu.VMEM((16, ROWS, EIGHTH), BF16),
            pltpu.VMEM((128, 256), BF16),
            pltpu.VMEM((128, 64), BF16),
            pltpu.SMEM((REQUESTS,), jnp.int32),
            dma((16,)), dma((4,)), dma((2,)), dma((16,)), dma((36,)), dma((2,)),
        ],
        compiler_params=pltpu.CompilerParams(
            collective_id=0, has_side_effects=True, vmem_limit_bytes=56 * 1024 * 1024
        ),
        cost_estimate=pl.CostEstimate(
            flops=5_000_000_000, bytes_accessed=14_000_000, transcendentals=400_000
        ),
    )(
        queries, cached_keys, cached_values, lengths, norm_gain.reshape(1, MODEL_WIDTH),
        expert_ids.T, gates.T, gate_proj, up_proj, down_proj,
    )


def solution(mesh):
    placed = (
        P(("grp", "tp"), None),
        P(("grp", "tp"), None, None),
        P(("grp", "tp"), None, None),
        P(("grp", "tp")),
        P(),
        P(("grp", "tp"), None),
        P(("grp", "tp"), None),
        P("grp", None, "tp"),
        P("grp", None, "tp"),
        P("grp", "tp", None),
    )
    return jax.shard_map(
        local, mesh=mesh, in_specs=placed, out_specs=P(("grp", "tp"), "role"), check_vma=False
    )
```
